256 devices in a mesh: dp: 32 (over z_hi, x, core), mp: 8 (over y, z_lo).
Axes of the slice: x: 4, y: 4, z: 8 (z_hi: 4, z_lo: 2; z = z_hi * 2 + z_lo), core: 2. Of those that a mesh axis runs over, the one named last changes fastest.
Arguments:
- tokens: bfloat16 [4096, 8192], P('dp'), may hold values from -6 to 6
- cotangent: bfloat16 [4096, 8192], P('dp'), may hold values from -1.1953125 to 1.1953125
- gate_weight: bfloat16 [112, 5, 128, 128], P('mp', None, 'dp'), may hold values from -0.3125 to 0.3125
- up_weight: bfloat16 [112, 5, 128, 128], P('mp', None, 'dp'), may hold values from -0.3125 to 0.3125
- down_weight: bfloat16 [112, 5, 128, 128], P('mp', None, 'dp'), may hold values from -0.25 to 0.25
- low_in: bfloat16 [8192, 64], P('dp'), may hold values from -0.0625 to 0.0625
- low_mid: bfloat16 [128, 14336], P('dp', 'mp'), may hold values from -0.75 to 0.75
- down_low_in: bfloat16 [64, 14336], P('dp', 'mp'), may hold values from -0.046875 to 0.046875
- down_low_out: bfloat16 [64, 8192], P('dp', 'mp'), may hold values from -0.75 to 0.75
- up_order: int32 [112], replicated, may hold values from 0 to 111, as said below
- down_order: int32 [112], replicated, may hold values from 0 to 111, as said below
- up_rows: int32 [112, 5], replicated, may hold values from 0 to 63, as said below
- down_cols: int32 [112, 5], replicated, may hold values from 0 to 63, as said below
- up_count: int32 [112], replicated, may hold values from 1 to 5, as said below
- down_count: int32 [112], replicated, may hold values from 1 to 5, as said below
Outputs:
- layer_out: bfloat16 [4096, 8192], P('dp', 'mp')
- token_grad: bfloat16 [4096, 8192], P('dp', 'mp')
- gate_weight_grad: bfloat16 [112, 5, 128, 128], P('mp', None, 'dp')
- up_weight_grad: bfloat16 [112, 5, 128, 128], P('mp', None, 'dp')
- down_weight_grad: bfloat16 [112, 5, 128, 128], P('mp', None, 'dp')
- low_in_grad: bfloat16 [8192, 64], P('dp')
- low_mid_grad: bfloat16 [128, 14336], P('dp', 'mp')
- down_low_in_grad: bfloat16 [64, 14336], P('dp', 'mp')
- down_low_out_grad: bfloat16 [64, 8192], P('dp', 'mp')
The draws below stay inside these ranges and needn't reach their ends.
Inputs may be any that keep to these rules, and one draw needn't show every extreme that they name: up_order is a permutation of the hidden blocks. Slots g * 14 to (g + 1) * 14 - 1 form slot group g. down_order is a permutation of the hidden blocks. For any slot group a of up_order and slot group b of down_order, at most 2 hidden blocks lie in both, and some pair of groups shares exactly 2. `up_rows`: the 5 entries of a slot are distinct; only the first up_count[s] are used. `down_cols`: the 5 entries of a slot are distinct; only the first down_count[t] are used. `up_count`: the counts of every slot group of 14 consecutive slots add up to exactly 42. `down_count`: the counts of every slot group of 14 consecutive slots add up to exactly 42.
All inputs are finite; a program needn't handle non-finite values.
Results may differ from the reference program's by a relative error of at most 0.035.
Values may be sent and summed in bfloat16 or wider, within the bound.
No kernel may reach another device: no remote copies, remote signals or barrier semaphores. Data moves between devices by JAX's collectives and lax.ppermute only.
A program may use at most 128 MiB of HBM per device.

```python
import jax
import jax.numpy as jnp
from jax import lax

D = 8192
FF = 14336
BLK = 128
KMAX = 5
RANK = 64
TOK_DEV = 128
TOKENS = 4096
FB = 112
SLOTS_DEV = 14
MOVE_CAP = 2


def owners(key):
    groups = FB // SLOTS_DEV
    up_order = jax.random.permutation(jax.random.fold_in(key, 101), FB).astype(jnp.int32)
    shift_pool = jnp.arange(groups * MOVE_CAP, dtype=jnp.int32) // MOVE_CAP
    shifts = jax.random.permutation(jax.random.fold_in(key, 102), shift_pool)[:SLOTS_DEV]
    places = jax.random.permutation(jax.random.fold_in(key, 103), SLOTS_DEV).astype(jnp.int32)
    device = jnp.arange(groups, dtype=jnp.int32)[:, None]
    source = (device + shifts[None, :]) % groups * SLOTS_DEV + places[None, :]
    down_order = up_order[source.reshape(-1)]
    return (up_order, down_order.astype(jnp.int32))


def butterfly(key, order_ids):
    offsets = jnp.concatenate([jnp.zeros((1,), jnp.int32), 2 ** jnp.arange(KMAX - 1, dtype=jnp.int32)])
    subkeys = jax.random.split(key, FB)
    offset_picks = jax.vmap(lambda subkey: jax.random.permutation(subkey, offsets))(subkeys)
    base_block = order_ids % (D // BLK)
    return jnp.bitwise_xor(base_block[:, None], offset_picks).astype(jnp.int32)


def live_counts(key):
    groups = FB // SLOTS_DEV
    half_slots = SLOTS_DEV // 2
    first_half = jax.random.randint(key, (groups, half_slots), 1, KMAX + 1, dtype=jnp.int32)
    first_half = first_half.at[0, 0].set(KMAX)
    paired = jnp.concatenate([first_half, KMAX + 1 - first_half], axis=1)
    subkeys = jax.random.split(jax.random.fold_in(key, 5), groups)
    mixed_rows = jax.vmap(lambda subkey, row_values: jax.random.permutation(subkey, row_values))(subkeys, paired)
    return mixed_rows.reshape(-1).astype(jnp.int32)


def draw_up_order(key, part):
    shared = owners(key)
    return shared[0]


def draw_down_order(key, part):
    shared = owners(key)
    return shared[1]


def draw_up_rows(key, part):
    shared = owners(key)
    key = jax.random.fold_in(key, 21)
    return butterfly(key, shared[0])


def draw_down_cols(key, part):
    shared = owners(key)
    key = jax.random.fold_in(key, 23)
    return butterfly(key, shared[1])


def draw_up_count(key, part):
    key = jax.random.fold_in(key, 31)
    return live_counts(key)


def draw_down_count(key, part):
    key = jax.random.fold_in(key, 37)
    return live_counts(key)


def steps_of(rng, dims, cuts, smallest, largest):
    factor_of = 1.0
    for position, blocks in cuts:
        heights = jax.random.uniform(jax.random.fold_in(jax.random.fold_in(rng, 6), position), (blocks,), jnp.float32, smallest / len(cuts), largest / len(cuts))
        factor_of = factor_of * jnp.repeat(jnp.exp(heights), dims[position] // blocks).reshape((-1,) + (1,) * (len(dims) - 1 - position))
    return factor_of


def noise(rng, extent, width, bound, pieces=(), kind=jnp.bfloat16):
    result = width * jax.random.normal(rng, extent, jnp.float32)
    if pieces:
        result = result * steps_of(rng, extent, pieces, -0.22, 0.18)
    return jnp.clip(result, -bound, bound).astype(kind)


def setup_inputs(seed: int = 0) -> dict:
    keys = jax.random.split(jax.random.key(seed), 16)
    return {
        "tokens": noise(keys[0], (TOKENS, D), 1.0, 6.0, ((0, 32),)),
        "cotangent": noise(keys[1], (TOKENS, D), 0.2, 1.1953125, ((0, 32),)),
        "gate_weight": noise(keys[2], (FB, KMAX, BLK, BLK), ((KMAX + 1) * BLK // 2) ** -0.5, 0.3125, ((0, 8), (2, 32))),
        "up_weight": noise(keys[3], (FB, KMAX, BLK, BLK), ((KMAX + 1) * BLK // 2) ** -0.5, 0.3125, ((0, 8), (2, 32))),
        "down_weight": noise(keys[4], (FB, KMAX, BLK, BLK), (FF * (KMAX + 1) // (2 * (D // BLK))) ** -0.5, 0.25, ((0, 8), (2, 32))),
        "low_in": noise(keys[5], (D, RANK), D ** -0.5, 0.0625, ((0, 32),)),
        "low_mid": noise(keys[6], (2 * RANK, FF), RANK ** -0.5, 0.75, ((0, 32), (1, 8))),
        "down_low_in": noise(keys[7], (RANK, FF), FF ** -0.5, 0.046875, ((0, 32), (1, 8))),
        "down_low_out": noise(keys[8], (RANK, D), RANK ** -0.5, 0.75, ((0, 32), (1, 8))),
        "up_order": draw_up_order(jax.random.fold_in(keys[15], 71), 0),
        "down_order": draw_down_order(jax.random.fold_in(keys[15], 71), 0),
        "up_rows": draw_up_rows(jax.random.fold_in(keys[15], 71), 0),
        "down_cols": draw_down_cols(jax.random.fold_in(keys[15], 71), 0),
        "up_count": draw_up_count(jax.random.fold_in(keys[15], 71), 0),
        "down_count": draw_down_count(jax.random.fold_in(keys[15], 71), 0),
    }


def inverse_of(order_ids):
    count_all = order_ids.shape[0]
    return jnp.zeros((count_all,), jnp.int32).at[order_ids].set(jnp.arange(count_all, dtype=jnp.int32))


def scatter_blocks(products, targets, block_count):
    tok_rows = products.shape[0]
    flat_terms = products.reshape(tok_rows, -1, products.shape[-1]).transpose(1, 0, 2)
    summed = jax.ops.segment_sum(flat_terms, targets.reshape(-1), num_segments=block_count)
    return summed.transpose(1, 0, 2).reshape(tok_rows, -1)


def reference(tokens, cotangent, gate_weight, up_weight, down_weight, low_in, low_mid, down_low_in, down_low_out, up_order, down_order, up_rows, down_cols, up_count, down_count):
    block_count = D // BLK
    group_count = TOKENS // TOK_DEV
    depth_ids = jnp.arange(KMAX, dtype=jnp.int32)[None, :]
    up_live = (depth_ids < up_count[:, None]).astype(jnp.float32)[:, :, None, None]
    down_live = (depth_ids < down_count[:, None]).astype(jnp.float32)[:, :, None, None]
    gate_full = gate_weight.astype(jnp.float32) * up_live
    up_full = up_weight.astype(jnp.float32) * up_live
    down_full = down_weight.astype(jnp.float32) * down_live
    to_down = inverse_of(up_order)[down_order]
    to_up = inverse_of(down_order)[up_order]
    mid_gate = low_mid[:RANK]
    mid_up = low_mid[RANK:]

    def one_group(running, rows_pair):
        token_rows, grad_rows = rows_pair
        token_sel = token_rows.astype(jnp.float32).reshape(TOK_DEV, block_count, BLK)[:, up_rows, :]
        latent = jnp.dot(token_rows, low_in, preferred_element_type=jnp.float32).astype(jnp.bfloat16)
        gate_pre = jnp.einsum("tskr,skrc->tsc", token_sel, gate_full).reshape(TOK_DEV, FF)
        gate_pre = gate_pre + jnp.dot(latent, mid_gate, preferred_element_type=jnp.float32)
        up_pre = jnp.einsum("tskr,skrc->tsc", token_sel, up_full).reshape(TOK_DEV, FF)
        up_pre = up_pre + jnp.dot(latent, mid_up, preferred_element_type=jnp.float32)
        sigmoid_gate = jax.nn.sigmoid(gate_pre)
        active = gate_pre * sigmoid_gate
        hidden = (active * up_pre).astype(jnp.bfloat16)
        hidden_down = hidden.reshape(TOK_DEV, FB, BLK)[:, to_down, :].reshape(TOK_DEV, FF)
        latent_down = jnp.dot(hidden_down, down_low_in.T, preferred_element_type=jnp.float32).astype(jnp.bfloat16)
        hidden_wide = hidden_down.astype(jnp.float32).reshape(TOK_DEV, FB, BLK)
        out_terms = jnp.einsum("tsh,skhc->tskc", hidden_wide, down_full)
        layer_out = scatter_blocks(out_terms, down_cols, block_count)
        layer_out = (layer_out + jnp.dot(latent_down, down_low_out, preferred_element_type=jnp.float32)).astype(jnp.bfloat16)
        back_latent = jnp.dot(grad_rows, down_low_out.T, preferred_element_type=jnp.float32).astype(jnp.bfloat16)
        grad_sel = grad_rows.astype(jnp.float32).reshape(TOK_DEV, block_count, BLK)[:, down_cols, :]
        hidden_grad = jnp.einsum("tskc,skhc->tsh", grad_sel, down_full).reshape(TOK_DEV, FF)
        hidden_grad = (hidden_grad + jnp.dot(back_latent, down_low_in, preferred_element_type=jnp.float32)).astype(jnp.bfloat16)
        flowing = hidden_grad.reshape(TOK_DEV, FB, BLK)[:, to_up, :].reshape(TOK_DEV, FF).astype(jnp.float32)
        gate_grad = (flowing * up_pre * sigmoid_gate * (1.0 + gate_pre * (1.0 - sigmoid_gate))).astype(jnp.bfloat16)
        up_grad = (flowing * active).astype(jnp.bfloat16)
        latent_grad = jnp.dot(gate_grad, mid_gate.T, preferred_element_type=jnp.float32)
        latent_grad = (latent_grad + jnp.dot(up_grad, mid_up.T, preferred_element_type=jnp.float32)).astype(jnp.bfloat16)
        gate_wide = gate_grad.astype(jnp.float32).reshape(TOK_DEV, FB, BLK)
        up_wide = up_grad.astype(jnp.float32).reshape(TOK_DEV, FB, BLK)
        input_terms = jnp.einsum("tsc,skrc->tskr", gate_wide, gate_full) + jnp.einsum("tsc,skrc->tskr", up_wide, up_full)
        token_grad = scatter_blocks(input_terms, up_rows, block_count)
        token_grad = (token_grad + jnp.dot(latent_grad, low_in.T, preferred_element_type=jnp.float32)).astype(jnp.bfloat16)
        partials = (
            jnp.einsum("tskr,tsc->skrc", token_sel, gate_wide) * up_live,
            jnp.einsum("tskr,tsc->skrc", token_sel, up_wide) * up_live,
            jnp.einsum("tsh,tskc->skhc", hidden_wide, grad_sel) * down_live,
            jnp.dot(token_rows.T, latent_grad, preferred_element_type=jnp.float32),
            jnp.concatenate([jnp.dot(latent.T, gate_grad, preferred_element_type=jnp.float32), jnp.dot(latent.T, up_grad, preferred_element_type=jnp.float32)], axis=0),
            jnp.dot(back_latent.T, hidden_down, preferred_element_type=jnp.float32),
            jnp.dot(latent_down.T, grad_rows, preferred_element_type=jnp.float32),
        )
        running = tuple(total_now + lax.optimization_barrier(portion.astype(jnp.bfloat16)).astype(jnp.float32) for total_now, portion in zip(running, partials))
        return running, (layer_out, token_grad)

    start_totals = (
        jnp.zeros((FB, KMAX, BLK, BLK), jnp.float32),
        jnp.zeros((FB, KMAX, BLK, BLK), jnp.float32),
        jnp.zeros((FB, KMAX, BLK, BLK), jnp.float32),
        jnp.zeros((D, RANK), jnp.float32),
        jnp.zeros((2 * RANK, FF), jnp.float32),
        jnp.zeros((RANK, FF), jnp.float32),
        jnp.zeros((RANK, D), jnp.float32),
    )
    grouped = (tokens.reshape(group_count, TOK_DEV, D), cotangent.reshape(group_count, TOK_DEV, D))
    running, stacked = lax.scan(one_group, start_totals, grouped)
    layer_out = stacked[0].reshape(TOKENS, D)
    token_grad = stacked[1].reshape(TOKENS, D)
    finals = tuple(total_now.astype(jnp.bfloat16) for total_now in running)
    return (layer_out, token_grad, finals[0], finals[1], finals[2], finals[3], finals[4], finals[5], finals[6])
```

```python
import jax
import jax.numpy as jnp
from jax import lax
from jax.experimental import pallas as pl
from jax.experimental.pallas import tpu as pltpu
from jax.sharding import Mesh, PartitionSpec as P

F32 = jnp.float32
BF16 = jnp.bfloat16
I32 = jnp.int32
DP = ("zh", "x", "core")
MP = ("y", "zl")
NDP, NMP = 32, 8
SLOTS, DEPTH, BLK = 14, 5, 128
LIVE = 42
RANK = 64
COLS = 64
SHARE = COLS // NMP
CAP = 2
VMEM_LIMIT = 58 * 2**20

GATE, MID, UP, DOWN, DLIN, LOWIN, PACK = 0, 42, 56, 100, 144, 152, 184
GRAD = 152

U_ROW, U_SLOT, D_COL, D_SLOT = 0, 48, 96, 144
U_KEY, D_KEY, U_POS, D_POS = 192, 264, 336, 408
SEND_A, SEND_B, GOT_A, GOT_B, WHO, META = 480, 496, 512, 528, 544, 560


def dot(a, b):
    return lax.dot_general(a, b, (((1,), (0,)), ((), ())), preferred_element_type=F32)


def dot_t(a, b):
    return lax.dot_general(a, b, (((1,), (1,)), ((), ())), preferred_element_type=F32)


def turned(a):
    return a.astype(F32).T.astype(BF16)


def span(start):
    return pl.ds(pl.multiple_of(start * BLK, BLK), BLK)


def call(body, out_shapes, operands, scalars, scratch=()):
    vmem = pl.BlockSpec(memory_space=pltpu.VMEM)
    smem = pl.BlockSpec(memory_space=pltpu.SMEM)
    return pl.pallas_call(
        body,
        out_shape=out_shapes,
        in_specs=[smem] * len(scalars) + [vmem] * len(operands),
        out_specs=jax.tree.map(lambda _: vmem, out_shapes),
        scratch_shapes=list(scratch),
        compiler_params=pltpu.CompilerParams(vmem_limit_bytes=VMEM_LIMIT),
    )(*scalars, *operands)


def shape(*dims, dtype=BF16):
    return jax.ShapeDtypeStruct(dims, dtype)


def pack_body(up_count, down_count, who, gate_w, up_w, down_w, extra, out):
    mine = who[0] * SLOTS
    for pad in (UP + 42, UP + 43, DOWN + 42, DOWN + 43):
        out[pad] = jnp.zeros((4, BLK), BF16)

    def put(weight, counts, base):
        at = jnp.int32(base)
        for s in range(SLOTS):
            count = counts[mine + s]
            for k in range(DEPTH):
                out[at] = weight[s, k]
                at = at + (k < count).astype(I32)

    put(gate_w, up_count, GATE)
    put(up_w, up_count, UP)
    put(down_w, down_count, DOWN)
    for s in range(SLOTS):
        out[MID + s] = extra[s]
    for e in range(PACK - DLIN):
        out[DLIN + e] = extra[SLOTS + e]


def back_latent_body(meta, got, cot, perm2, out):
    mine = meta[WHO] * SHARE
    rows = dot(perm2[...], got[...].reshape(512, BLK)).astype(BF16)
    acc = jnp.zeros((BLK, RANK), F32)
    for e in range(SHARE):
        acc = acc + dot_t(cot[:, span(mine + e)], rows[e * RANK : (e + 1) * RANK])
    out[...] = jnp.concatenate([acc, jnp.zeros_like(acc)], axis=1).astype(BF16)


def forward_body(
    meta, got, tok, cot, back, perm, perm2,
    send, act, w_gu, w_d, mid, dlin, lat, low_share, hid, hgrad,
):
    def rows(block):
        return got[:, 4 * block : 4 * block + 16, :].reshape(512, BLK)

    def pair(first, second):
        joined = jnp.concatenate([rows(first), rows(second)], axis=1)
        return dot(perm[...], joined).astype(BF16)

    for g in range(11):
        both = pair(GATE + 4 * g, UP + 4 * g)
        for jj in range(4):
            piece = both[jj * BLK : (jj + 1) * BLK]
            if 4 * g + jj < LIVE:
                w_gu[4 * g + jj] = piece
            else:
                mid[4 * g + jj - LIVE] = piece[:, :BLK]
    w_gu[LIVE] = jnp.zeros((BLK, 2 * BLK), BF16)
    tiles = [("m", i) for i in range(2, 14, 4)] + [("d", i) for i in range(0, 44, 4)]
    for a, b in zip(tiles[0::2], tiles[1::2]):
        at = [(MID if t == "m" else DOWN) + i for t, i in (a, b)]
        both = pair(*at)
        for jj in range(4):
            for half, (t, i) in enumerate((a, b)):
                piece = both[jj * BLK : (jj + 1) * BLK, half * BLK : (half + 1) * BLK]
                if t == "m":
                    mid[i + jj] = piece
                elif i + jj < LIVE:
                    w_d[i + jj] = piece
    w_d[LIVE] = jnp.zeros((BLK, BLK), BF16)
    joined = jnp.concatenate([rows(DLIN), rows(DLIN + 4)], axis=1)
    both = dot(perm2[...], joined).astype(BF16)
    for t in range(SLOTS):
        dlin[t] = both[(t % 8) * RANK : (t % 8 + 1) * RANK, (t // 8) * BLK : (t // 8 + 1) * BLK]

    acc0 = jnp.zeros((BLK, BLK), F32)
    acc1 = jnp.zeros((BLK, BLK), F32)
    for d in range(NDP):
        low = got[d, 4 * LOWIN : 4 * PACK, :]
        acc0 = acc0 + dot(tok[:, 2 * d * BLK : (2 * d + 1) * BLK], low)
        acc1 = acc1 + dot(tok[:, (2 * d + 1) * BLK : (2 * d + 2) * BLK], low)
    latent = (acc0[:, :RANK] + acc1[:, RANK:]).astype(BF16)
    total = back[0].astype(F32)
    for i in range(1, NMP):
        total = total + back[i].astype(F32)
    back_latent = total[:, :RANK].astype(BF16)
    lat[0] = latent
    lat[1] = back_latent
    for i in range(4):
        low_share[i] = got[4 * meta[WHO] + i, 4 * LOWIN : 4 * PACK, :]

    for t in range(SLOTS):
        acc = dot(back_latent, dlin[t])
        for k in range(DEPTH):
            p = DEPTH * t + k
            acc = acc + dot_t(cot[:, span(meta[D_KEY + p])], w_d[meta[D_POS + p]])
        hgrad[t] = acc.astype(BF16)
    for s in range(SLOTS):
        acc = jnp.concatenate([dot(latent, mid[s, :RANK]), dot(latent, mid[s, RANK:])], axis=1)
        for k in range(DEPTH):
            p = DEPTH * s + k
            acc = acc + dot(tok[:, span(meta[U_KEY + p])], w_gu[meta[U_POS + p]])
        gate, up = acc[:, :BLK], acc[:, BLK:]
        sig = jax.nn.sigmoid(gate)
        active = gate * sig
        hid[s] = (active * up).astype(BF16)
        act[s, :, :BLK] = up * sig * (1.0 + gate * (1.0 - sig))
        act[s, :, BLK:] = active
    for lane in range(NMP * CAP):
        send[lane // CAP, lane % CAP] = hid[meta[SEND_A + lane]]
        send[lane // CAP, CAP + lane % CAP] = hgrad[meta[SEND_B + lane]]


def grads_body(
    meta, got, act, mid, dlin, lat, tok_t, cot, perm, perm2,
    grad, gu, hd, part, hd_t, midg, ding,
):
    latent_t = turned(jnp.concatenate([lat[0], lat[1]], axis=1))
    lat_sum = jnp.zeros((BLK, RANK), F32)
    down_sum = jnp.zeros((BLK, RANK), F32)
    for s in range(SLOTS):
        lane = meta[GOT_B + s]
        flow = got[lane // CAP, CAP + lane % CAP].astype(F32)
        gg = (flow * act[s, :, :BLK]).astype(BF16)
        ug = (flow * act[s, :, BLK:]).astype(BF16)
        both = jnp.concatenate([gg, ug], axis=1)
        gu[s] = both
        lat_sum = lat_sum + dot_t(gg, mid[s, :RANK]) + dot_t(ug, mid[s, RANK:])
        two = dot(latent_t[:RANK], both).astype(BF16)
        midg[s] = jnp.concatenate([two[:, :BLK], two[:, BLK:]], axis=0)
        lane = meta[GOT_A + s]
        h = got[lane // CAP, lane % CAP]
        hd[s] = h
        hd_t[s] = turned(h)
        down_sum = down_sum + dot_t(h, dlin[s])
        ding[s] = dot(latent_t[RANK:], h).astype(BF16)
    part[...] = jnp.concatenate([lat_sum, down_sum], axis=1).astype(BF16)

    def store(tile, rows):
        grad[:, 4 * tile : 4 * tile + 16, :] = rows.reshape(NDP, 16, BLK)

    def pair(first, second, left, right):
        both = dot(perm[...], jnp.concatenate([left, right], axis=1)).astype(BF16)
        store(first, both[:, :BLK])
        store(second, both[:, BLK:])

    zero = jnp.zeros((BLK, BLK), BF16)
    for g in range(11):
        pieces = []
        for j in range(4 * g, 4 * g + 4):
            if j < LIVE:
                piece = dot(tok_t[meta[U_ROW + j]], gu[meta[U_SLOT + j]]).astype(BF16)
            else:
                piece = jnp.concatenate([midg[j - LIVE], zero], axis=1)
            pieces.append(piece)
        both = dot(perm[...], jnp.concatenate(pieces, axis=0)).astype(BF16)
        store(GATE + 4 * g, both[:, :BLK])
        store(UP + 4 * g, both[:, BLK:])

    def tile_of(kind, i):
        pieces = []
        for j in range(i, i + 4):
            if kind == "m":
                pieces.append(midg[j])
            elif j < LIVE:
                cols = cot[:, span(meta[D_COL + j])]
                pieces.append(dot(hd_t[meta[D_SLOT + j]], cols).astype(BF16))
            else:
                pieces.append(zero)
        return jnp.concatenate(pieces, axis=0)

    tiles = [("m", i) for i in range(2, 14, 4)] + [("d", i) for i in range(0, 44, 4)]
    for a, b in zip(tiles[0::2], tiles[1::2]):
        at = [(MID if t == "m" else DOWN) + i for t, i in (a, b)]
        pair(*at, tile_of(*a), tile_of(*b))
    none = jnp.zeros((RANK, BLK), BF16)
    left = jnp.concatenate([ding[t] for t in range(8)], axis=0)
    right = jnp.concatenate([ding[t] for t in range(8, SLOTS)] + [none, none], axis=0)
    both = dot(perm2[...], jnp.concatenate([left, right], axis=1)).astype(BF16)
    store(DLIN, both[:, :BLK])
    store(DLIN + 4, both[:, BLK:])


def token_part_body(meta, gu, w_gu, out, acc):
    acc[...] = jnp.zeros_like(acc)
    for j in range(LIVE):
        r = meta[U_ROW + j]
        acc[r] = acc[r] + dot_t(gu[meta[U_SLOT + j]], w_gu[j])
    for b in range(COLS):
        out[b // SHARE, b % SHARE] = acc[b].astype(BF16)


def out_part_body(meta, hd, w_d, out, acc):
    acc[...] = jnp.zeros_like(acc)
    for j in range(LIVE):
        c = meta[D_COL + j]
        acc[c] = acc[c] + dot(hd[meta[D_SLOT + j]], w_d[j])
    for b in range(COLS):
        out[b // SHARE, b % SHARE] = acc[b].astype(BF16)


def small_grads_body(meta, parts, tok_t, cot, perm2, latents, grad):
    total = parts[0].astype(F32)
    for i in range(1, NMP):
        total = total + parts[i].astype(F32)
    total = total.astype(BF16)
    latents[0] = total[:, :RANK]
    latents[1] = total[:, RANK:]
    who = meta[WHO]
    rows = pl.ds(pl.multiple_of((who % 4) * 32, 32), 32)
    pieces = [tok_t[2 * d + who // 4, rows, :] for d in range(NDP)]
    low = dot(jnp.concatenate(pieces, axis=0), total[:, :RANK]).reshape(NDP, 32, RANK)
    low = jnp.concatenate([low[:, :16], low[:, 16:]], axis=2)
    grad[:, :16, :] = low.astype(BF16)
    down_t = turned(total)[RANK:]
    pieces = [dot(down_t, cot[:, span(who * SHARE + e)]).astype(BF16) for e in range(SHARE)]
    rows = dot(perm2[...], jnp.concatenate(pieces, axis=0)).astype(BF16)
    grad[:, 16:, :] = rows.reshape(NDP, 16, BLK)


def token_out_body(got, latents, low_share, out):
    latent = latents[0]
    for e in range(SHARE):
        total = got[0, e].astype(F32)
        for i in range(1, NMP):
            total = total + got[i, e].astype(F32)
        low = low_share[e // 2]
        low = low[:, :RANK] if e % 2 == 0 else low[:, RANK:]
        out[:, e * BLK : (e + 1) * BLK] = (total + dot_t(latent, low)).astype(BF16)


def layer_out_body(got, latents, dlout, perm2, out):
    latent = latents[1]
    rows = dot(perm2[...], dlout[...].reshape(512, BLK)).astype(BF16)
    for e in range(SHARE):
        total = got[0, e].astype(F32)
        for i in range(1, NMP):
            total = total + got[i, e].astype(F32)
        low = dot(latent, rows[e * RANK : (e + 1) * RANK])
        out[:, e * BLK : (e + 1) * BLK] = (total + low).astype(BF16)


def final_body(up_count, down_count, who, got, gate_o, up_o, down_o, mid_o, tail, red):
    total = got[0].astype(F32)
    for i in range(1, 4):
        total = total + got[i].astype(F32)
    red[...] = total.astype(BF16)
    mine = who[0] * SLOTS
    zero = jnp.zeros((4, BLK), BF16)

    def put(out, counts, base):
        at = jnp.int32(base)
        for s in range(SLOTS):
            count = counts[mine + s]
            for k in range(DEPTH):
                out[s, k] = jnp.where(k < count, red[at], zero)
                at = at + (k < count).astype(I32)

    put(gate_o, up_count, GATE)
    put(up_o, up_count, UP)
    put(down_o, down_count, DOWN)
    for s in range(SLOTS):
        mid_o[:, s * BLK : (s + 1) * BLK] = red[MID + s]
    for e in range(8):
        tail[e] = red[DLIN + e]


def lookup(table_ids, positions):
    span_ids = jnp.arange(table_ids.shape[0], dtype=I32)
    return jnp.sum(jnp.where(positions[..., None] == span_ids, table_ids, 0), axis=-1)


def own_rows(table_ids, mine):
    return lax.dynamic_slice_in_dim(table_ids, mine * SLOTS, SLOTS, 0)


def inverse_of(order_ids):
    ids = jnp.arange(order_ids.shape[0], dtype=I32)
    return jnp.sum(jnp.where(order_ids[None, :] == ids[:, None], ids[None, :], 0), axis=1)


def send_table(owner, peer, rank, local_slot, mine):
    lanes = jnp.arange(NMP * CAP, dtype=I32)
    target = peer * CAP + rank
    matched = (owner[None, :] == mine) & (target[None, :] == lanes[:, None])
    return jnp.sum(jnp.where(matched, local_slot[None, :], 0), axis=1)


def live_table(count, keys):
    live = (jnp.arange(DEPTH, dtype=I32)[None, :] < count[:, None]).reshape(-1)
    ids = jnp.arange(SLOTS * DEPTH, dtype=I32)
    place = jnp.sum(jnp.where((ids[None, :] < ids[:, None]) & live[None, :], 1, 0), axis=1)
    hit = (jnp.arange(LIVE, dtype=I32)[:, None] == place[None, :]) & live[None, :]
    flat = keys.reshape(-1)
    of_key = jnp.sum(jnp.where(hit, flat[None, :], 0), axis=1)
    of_slot = jnp.sum(jnp.where(hit, (ids // DEPTH)[None, :], 0), axis=1)
    return of_key, of_slot, flat, jnp.where(live, place, LIVE)


def tables(mine, up_order, down_order, up_rows, down_cols, up_count, down_count):
    slot_ids = jnp.arange(up_order.shape[0], dtype=I32)
    source = lookup(inverse_of(up_order), down_order)
    from_device, to_device = source // SLOTS, slot_ids // SLOTS
    earlier = (
        (from_device[None, :] == from_device[:, None])
        & (to_device[None, :] == to_device[:, None])
        & (slot_ids[None, :] < slot_ids[:, None])
    )
    rank = jnp.sum(earlier.astype(I32), axis=1)
    send_a = send_table(from_device, to_device, rank, source % SLOTS, mine)
    got_a = own_rows(from_device * CAP + rank, mine)
    send_b = send_table(to_device, from_device, rank, slot_ids % SLOTS, mine)
    blocks_down = lookup(inverse_of(down_order), own_rows(up_order, mine))
    got_b = lookup(to_device * CAP + rank, blocks_down)
    u = live_table(own_rows(up_count, mine), own_rows(up_rows, mine))
    d = live_table(own_rows(down_count, mine), own_rows(down_cols, mine))
    fields = [
        (U_ROW, u[0]), (U_SLOT, u[1]), (D_COL, d[0]), (D_SLOT, d[1]), (U_KEY, u[2]), (D_KEY, d[2]),
        (U_POS, u[3]), (D_POS, d[3]), (SEND_A, send_a), (SEND_B, send_b), (GOT_A, got_a),
        (GOT_B, got_b), (WHO, mine.reshape(1)),
    ]
    ends = [start for start, _ in fields[1:]] + [META]
    padded = [jnp.pad(v, (0, end - start - v.shape[0])) for (start, v), end in zip(fields, ends)]
    return jnp.concatenate(padded)


def permutations():
    r = jnp.arange(512, dtype=I32)
    q_device, q_rest = r // 16, r % 16
    device = (q_device % 4) * 8 + q_device // 4
    row4 = lambda d, rest: (rest // 4) * BLK + 4 * d + rest % 4
    row2 = lambda d, rest: (rest // 2) * RANK + 2 * d + rest % 2
    mat = lambda src: (src[:, None] == r[None, :]).astype(BF16)
    take = mat(row4(q_device, q_rest)).T
    take2 = mat(row2(q_device, q_rest)).T
    give = mat(row4(device, q_rest))
    give2 = mat(row2(device, q_rest))
    give2_plain = mat(row2(q_device, q_rest))
    return take, take2, give, give2, give2_plain


def spread(x, axis, n):
    return lax.all_to_all(jnp.broadcast_to(x[None], (n,) + x.shape), axis, 0, 0, tiled=True)


def local(
    tokens, cotangent, gate_weight, up_weight, down_weight, low_in, low_mid, down_low_in,
    down_low_out, up_order, down_order, up_rows, down_cols, up_count, down_count,
):
    mine = lax.axis_index(MP).astype(I32)
    who = mine.reshape(1)
    mid_rows = low_mid.reshape(4, SLOTS, BLK).transpose(1, 0, 2)
    dlin_rows = jnp.pad(
        down_low_in.reshape(2, SLOTS, BLK).transpose(1, 0, 2).reshape(2 * SLOTS, BLK), ((0, 4), (0, 0))
    ).reshape(8, 4, BLK)
    low_rows = jnp.concatenate([low_in[:BLK], low_in[BLK:]], axis=1).reshape(32, 4, BLK)
    extra = jnp.concatenate([mid_rows, dlin_rows, low_rows], axis=0)
    packed = call(
        pack_body, shape(PACK, 4, BLK), (gate_weight, up_weight, down_weight, extra),
        (up_count, down_count, who),
    )
    gathered = lax.all_gather(packed.reshape(4 * PACK, BLK), DP)

    meta = tables(mine, up_order, down_order, up_rows, down_cols, up_count, down_count)
    take, take2, give, give2, give2_plain = permutations()
    tok_t = tokens.reshape(BLK, COLS, BLK).transpose(1, 2, 0)
    dlout = down_low_out.reshape(2, SHARE, BLK).transpose(1, 0, 2).reshape(16, BLK)
    dlout = spread(dlout, DP, NDP)
    back = call(back_latent_body, shape(BLK, BLK), (dlout, cotangent, take2), (meta,))
    back = spread(back, MP, NMP)

    send, act, w_gu, w_d, mid, dlin, lat, low_share = call(
        forward_body,
        (
            shape(NMP, 2 * CAP, BLK, BLK), shape(SLOTS, BLK, 2 * BLK, dtype=F32),
            shape(LIVE + 1, BLK, 2 * BLK), shape(LIVE + 1, BLK, BLK), shape(SLOTS, BLK, BLK),
            shape(SLOTS, RANK, BLK), shape(2, BLK, RANK), shape(4, BLK, BLK),
        ),
        (gathered, tokens, cotangent, back, take, take2),
        (meta,),
        (pltpu.VMEM((SLOTS, BLK, BLK), BF16), pltpu.VMEM((SLOTS, BLK, BLK), BF16)),
    )
    got = lax.all_to_all(send, MP, 0, 0, tiled=True)

    grad, gu, hd, part = call(
        grads_body,
        (
            shape(NDP, 4 * GRAD, BLK), shape(SLOTS, BLK, 2 * BLK), shape(SLOTS, BLK, BLK),
            shape(BLK, BLK),
        ),
        (got, act, mid, dlin, lat, tok_t, cotangent, give, give2),
        (meta,),
        (
            pltpu.VMEM((SLOTS, BLK, BLK), BF16), pltpu.VMEM((SLOTS, BLK, BLK), BF16),
            pltpu.VMEM((SLOTS, RANK, BLK), BF16),
        ),
    )
    grad = lax.psum_scatter(
        grad.reshape(NDP * 4 * GRAD, BLK), ("x", "core"), scatter_dimension=0, tiled=True
    )
    parts = spread(part, MP, NMP)
    latents, small = call(
        small_grads_body, (shape(2, BLK, RANK), shape(NDP, 32, BLK)),
        (parts, tok_t, cotangent, give2_plain), (meta,),
    )

    acc = pltpu.VMEM((COLS, BLK, BLK), F32)
    columns = shape(NMP, SHARE, BLK, BLK)
    token_part = call(token_part_body, columns, (gu, w_gu), (meta,), (acc,))
    token_got = lax.all_to_all(token_part, MP, 0, 0, tiled=True)
    out_part = call(out_part_body, columns, (hd, w_d), (meta,), (acc,))
    out_got = lax.all_to_all(out_part, MP, 0, 0, tiled=True)
    token_grad = call(
        token_out_body, shape(BLK, SHARE * BLK), (token_got, latents, low_share), ()
    )
    layer_out = call(
        layer_out_body, shape(BLK, SHARE * BLK), (out_got, latents, dlout, take2), ()
    )

    small = lax.all_to_all(small, DP, 0, 0, tiled=True)
    small = jnp.sum(small.astype(F32), axis=0).astype(BF16)
    low_g = spread(small[:16], MP, NMP)
    low_g = jnp.concatenate([low_g[:, :, :RANK], low_g[:, :, RANK:]], axis=1)
    low_in_grad = low_g.reshape(2 * BLK, RANK)
    dlout_g = small[16:].reshape(SHARE, 2, BLK).transpose(1, 0, 2).reshape(2, SHARE * BLK)
    grad = lax.all_to_all(grad.reshape(4, 4 * GRAD, BLK), "zh", 0, 0, tiled=True)
    wide = shape(SLOTS, DEPTH, 4, BLK)
    gate_g, up_g, down_g, mid_g, tail = call(
        final_body, (wide, wide, wide, shape(4, SLOTS * BLK), shape(8, 4, BLK)),
        (grad.reshape(4, GRAD, 4, BLK),), (up_count, down_count, who),
        (pltpu.VMEM((GRAD, 4, BLK), BF16),),
    )
    dlin_g = tail.reshape(16, 2, BLK)[:SLOTS].transpose(1, 0, 2).reshape(2, SLOTS * BLK)
    return layer_out, token_grad, gate_g, up_g, down_g, low_in_grad, mid_g, dlin_g, dlout_g


def solution(mesh):
    fine = Mesh(mesh.devices.reshape(4, 4, 2, 4, 2), DP + MP)
    rows, both, blocks = P(DP, None), P(DP, MP), P(MP, None, DP, None)
    in_specs = (rows, rows, blocks, blocks, blocks, rows, both, both, both) + (P(),) * 6
    out_specs = (both, both, blocks, blocks, blocks, rows, both, both, both)
    return jax.shard_map(local, mesh=fine, in_specs=in_specs, out_specs=out_specs, check_vma=False)
```

```python
import jax
import jax.numpy as jnp
from jax import lax
from jax.experimental import pallas as pl
from jax.experimental.pallas import tpu as pltpu
from jax.sharding import Mesh, PartitionSpec as P

F32 = jnp.float32
BF16 = jnp.bfloat16
I32 = jnp.int32
DP = ("zh", "x", "core")
MP = ("y", "zl")
NDP, NMP = 32, 8
SLOTS, DEPTH, BLK = 14, 5, 128
LIVE = 42
RANK = 64
COLS = 64
SHARE = COLS // NMP
CAP = 2
NY = 4
BACK_LOW = CAP * BLK
BACK_SUM = BACK_LOW + CAP * RANK
BACK_ROWS = BACK_SUM + BLK
VMEM_LIMIT = 58 * 2**20

GATE, MID, UP, LOWIN, PACK_A = 0, 42, 56, 100, 132
DOWN, DLIN, DLOUT, PACK_B = 0, 44, 52, 56
GRAD_A, GRAD = 100, 152

U_ROW, U_SLOT, D_COL, D_SLOT = 0, 48, 96, 144
U_KEY, D_KEY, U_POS, D_POS = 192, 264, 336, 408
SEND_A, SEND_B, GOT_A, GOT_B, WHO, META = 480, 496, 512, 528, 544, 560


def dot(a, b):
    return lax.dot_general(a, b, (((1,), (0,)), ((), ())), preferred_element_type=F32)


def dot_t(a, b):
    return lax.dot_general(a, b, (((1,), (1,)), ((), ())), preferred_element_type=F32)


def turned(a):
    return a.astype(F32).T.astype(BF16)


def span(start):
    return pl.ds(pl.multiple_of(start * BLK, BLK), BLK)


def call(body, out_shapes, operands, scalars, scratch=()):
    vmem = pl.BlockSpec(memory_space=pltpu.VMEM)
    smem = pl.BlockSpec(memory_space=pltpu.SMEM)
    return pl.pallas_call(
        body,
        out_shape=out_shapes,
        in_specs=[smem] * len(scalars) + [vmem] * len(operands),
        out_specs=jax.tree.map(lambda _: vmem, out_shapes),
        scratch_shapes=list(scratch),
        compiler_params=pltpu.CompilerParams(vmem_limit_bytes=VMEM_LIMIT),
    )(*scalars, *operands)


def shape(*dims, dtype=BF16):
    return jax.ShapeDtypeStruct(dims, dtype)


def pack_body(up_count, down_count, who, gate_w, up_w, down_w, mid, low, dlin, dlout, first, second):
    mine = who[0] * SLOTS
    for pad in (UP + 42, UP + 43):
        first[pad] = jnp.zeros((4, BLK), BF16)
    for pad in (DOWN + 42, DOWN + 43):
        second[pad] = jnp.zeros((4, BLK), BF16)

    def put(out, weight, counts, base):
        at = jnp.int32(base)
        for s in range(SLOTS):
            count = counts[mine + s]
            for k in range(DEPTH):
                out[at] = weight[s, k]
                at = at + (k < count).astype(I32)

    put(second, down_w, down_count, DOWN)
    put(first, gate_w, up_count, GATE)
    put(first, up_w, up_count, UP)
    for s in range(SLOTS):
        first[MID + s] = mid[s]
    for e in range(32):
        first[LOWIN + e] = low[e]
    for e in range(8):
        second[DLIN + e] = dlin[e]
    for e in range(4):
        second[DLOUT + e] = dlout[e]


def hidden_grad_body(meta, got, cot, perm, perm2, send, w_d, dlin, dlout, hgrad):
    def rows(block):
        return got[:, 4 * block : 4 * block + 16, :].reshape(512, BLK)

    for g in range(0, 11, 2):
        blocks = [DOWN + 4 * i for i in (g, g + 1) if i < 11]
        both = dot(perm[...], jnp.concatenate([rows(b) for b in blocks], axis=1)).astype(BF16)
        for half in range(len(blocks)):
            for jj in range(4):
                j = 4 * (g + half) + jj
                if j < LIVE:
                    w_d[j] = both[jj * BLK : (jj + 1) * BLK, half * BLK : (half + 1) * BLK]
    w_d[LIVE] = jnp.zeros((BLK, BLK), BF16)
    joined = jnp.concatenate([rows(DLIN), rows(DLIN + 4)], axis=1)
    both = dot(perm2[...], joined).astype(BF16)
    for t in range(SLOTS):
        dlin[t] = both[(t % 8) * RANK : (t % 8 + 1) * RANK, (t // 8) * BLK : (t // 8 + 1) * BLK]
    who = meta[WHO] * SHARE
    low = dot(perm2[...], rows(DLOUT)).astype(BF16)
    dlout[...] = low
    total = jnp.zeros((BLK, RANK), F32)
    for e in range(SHARE):
        total = total + dot_t(cot[:, span(who + e)], low[e * RANK : (e + 1) * RANK])
    total = jnp.concatenate([total, jnp.zeros_like(total)], axis=1).astype(BF16)
    for t in range(SLOTS):
        acc = jnp.zeros((BLK, BLK), F32)
        for k in range(DEPTH):
            p = DEPTH * t + k
            acc = acc + dot_t(cot[:, span(meta[D_KEY + p])], w_d[meta[D_POS + p]])
        hgrad[t] = acc.astype(BF16)
    for lane in range(NMP * CAP):
        peer, c = lane // CAP, lane % CAP
        t = meta[SEND_B + lane]
        send[peer, c * BLK : (c + 1) * BLK] = hgrad[t]
        send[peer, BACK_LOW + c * RANK : BACK_LOW + (c + 1) * RANK] = dlin[t]
    for peer in range(NMP):
        send[peer, BACK_SUM:] = total


def forward_body(meta, got, tok, perm, send, act, w_gu, mid, lat, low_share, hid):
    def rows(block):
        return got[:, 4 * block : 4 * block + 16, :].reshape(512, BLK)

    def pair(first, second):
        joined = jnp.concatenate([rows(first), rows(second)], axis=1)
        return dot(perm[...], joined).astype(BF16)

    for g in range(11):
        both = pair(GATE + 4 * g, UP + 4 * g)
        for jj in range(4):
            piece = both[jj * BLK : (jj + 1) * BLK]
            if 4 * g + jj < LIVE:
                w_gu[4 * g + jj] = piece
            else:
                mid[4 * g + jj - LIVE] = piece[:, :BLK]
    w_gu[LIVE] = jnp.zeros((BLK, 2 * BLK), BF16)
    for a, b in ((2, 6), (10, 10)):
        both = pair(MID + a, MID + b)
        for half, i in enumerate((a, b)[: 1 + (a != b)]):
            for jj in range(4):
                mid[i + jj] = both[jj * BLK : (jj + 1) * BLK, half * BLK : (half + 1) * BLK]

    acc0 = jnp.zeros((BLK, BLK), F32)
    acc1 = jnp.zeros((BLK, BLK), F32)
    for d in range(NDP):
        low = got[d, 4 * LOWIN : 4 * PACK_A, :]
        acc0 = acc0 + dot(tok[:, 2 * d * BLK : (2 * d + 1) * BLK], low)
        acc1 = acc1 + dot(tok[:, (2 * d + 1) * BLK : (2 * d + 2) * BLK], low)
    latent = (acc0[:, :RANK] + acc1[:, RANK:]).astype(BF16)
    lat[...] = latent
    for i in range(4):
        low_share[i] = got[4 * meta[WHO] + i, 4 * LOWIN : 4 * PACK_A, :]

    for s in range(SLOTS):
        acc = jnp.concatenate([dot(latent, mid[s, :RANK]), dot(latent, mid[s, RANK:])], axis=1)
        for k in range(DEPTH):
            p = DEPTH * s + k
            acc = acc + dot(tok[:, span(meta[U_KEY + p])], w_gu[meta[U_POS + p]])
        gate, up = acc[:, :BLK], acc[:, BLK:]
        sig = jax.nn.sigmoid(gate)
        active = gate * sig
        hid[s] = (active * up).astype(BF16)
        act[s, :, :BLK] = up * sig * (1.0 + gate * (1.0 - sig))
        act[s, :, BLK:] = active
    for lane in range(NMP * CAP):
        send[lane // CAP, lane % CAP] = hid[meta[SEND_A + lane]]


def up_grads_body(
    meta, got, act, mid, lat, tok_t, perm, grad, gu, part, back_latent, midg, full, sem
):
    latent = lat[...]
    total = got[0, BACK_SUM:].astype(F32)
    for i in range(1, NMP):
        total = total + got[i, BACK_SUM:].astype(F32)
    back = total[:, :RANK].astype(BF16)
    back_latent[...] = back
    latent_t = turned(jnp.concatenate([latent, latent], axis=1))[:RANK]
    lat_sum = jnp.zeros((BLK, RANK), F32)
    for s in range(SLOTS):
        lane = meta[GOT_B + s]
        peer, c = lane // CAP, lane % CAP
        block = got[peer, span(c), :].astype(F32)
        at = pl.multiple_of(BACK_LOW + c * RANK, RANK)
        flow = (block + dot(back, got[peer, pl.ds(at, RANK), :])).astype(BF16).astype(F32)
        gg = (flow * act[s, :, :BLK]).astype(BF16)
        ug = (flow * act[s, :, BLK:]).astype(BF16)
        both = jnp.concatenate([gg, ug], axis=1)
        gu[s] = both
        lat_sum = lat_sum + dot_t(gg, mid[s, :RANK]) + dot_t(ug, mid[s, RANK:])
        two = dot(latent_t, both).astype(BF16)
        midg[s] = jnp.concatenate([two[:, :BLK], two[:, BLK:]], axis=0)
    part[...] = lat_sum

    def store(block, rows):
        full[:, 4 * block : 4 * block + 16, :] = rows.reshape(NDP, 16, BLK)

    zero = jnp.zeros((BLK, BLK), BF16)
    for g in range(11):
        pieces = []
        for j in range(4 * g, 4 * g + 4):
            if j < LIVE:
                piece = dot(tok_t[meta[U_ROW + j]], gu[meta[U_SLOT + j]]).astype(BF16)
            else:
                piece = jnp.concatenate([midg[j - LIVE], zero], axis=1)
            pieces.append(piece)
        both = dot(perm[...], jnp.concatenate(pieces, axis=0)).astype(BF16)
        store(GATE + 4 * g, both[:, :BLK])
        store(UP + 4 * g, both[:, BLK:])
    for i in (2, 6, 10):
        rows = jnp.concatenate([midg[i + jj] for jj in range(4)], axis=0)
        store(MID + i, dot(perm[...], rows).astype(BF16))
    copy = pltpu.make_async_copy(full, grad.at[:, : 4 * GRAD_A, :], sem)
    copy.start()
    copy.wait()


def down_grads_body(
    meta, got, dlin, back_latent, cot, perm, perm2, start, grad, hd, part, hd_t, ding, full, sem
):
    back = back_latent[...]
    back_t = turned(jnp.concatenate([back, back], axis=1))[:RANK]
    down_sum = jnp.zeros((BLK, RANK), F32)
    for t in range(SLOTS):
        lane = meta[GOT_A + t]
        h = got[lane // CAP, lane % CAP]
        hd[t] = h
        hd_t[t] = turned(h)
        down_sum = down_sum + dot_t(h, dlin[t])
        ding[t] = dot(back_t, h).astype(BF16)
    part[...] = down_sum

    def store(block, rows):
        full[:, 4 * block : 4 * block + 16, :] = rows.reshape(NDP, 16, BLK)

    zero = jnp.zeros((BLK, BLK), BF16)

    def tile_of(g):
        pieces = []
        for j in range(4 * g, 4 * g + 4):
            if j < LIVE:
                cols = cot[:, span(meta[D_COL + j])]
                pieces.append(dot(hd_t[meta[D_SLOT + j]], cols).astype(BF16))
            else:
                pieces.append(zero)
        return jnp.concatenate(pieces, axis=0)

    for g in range(0, 11, 2):
        tiles = [i for i in (g, g + 1) if i < 11]
        both = dot(perm[...], jnp.concatenate([tile_of(i) for i in tiles], axis=1)).astype(BF16)
        for half, i in enumerate(tiles):
            store(DOWN + 4 * i, both[:, half * BLK : (half + 1) * BLK])
    none = jnp.zeros((RANK, BLK), BF16)
    left = jnp.concatenate([ding[t] for t in range(8)], axis=0)
    right = jnp.concatenate([ding[t] for t in range(8, SLOTS)] + [none, none], axis=0)
    both = dot(perm2[...], jnp.concatenate([left, right], axis=1)).astype(BF16)
    store(DLIN, both[:, :BLK])
    store(DLIN + 4, both[:, BLK:])
    copy = pltpu.make_async_copy(full, grad.at[:, 4 * GRAD_A :, :], sem)
    copy.start()
    copy.wait()


def token_part_body(meta, gu, w_gu, keep, pass_on, acc):
    acc[...] = jnp.zeros_like(acc)
    for j in range(LIVE):
        r = meta[U_ROW + j]
        acc[r] = acc[r] + dot_t(gu[meta[U_SLOT + j]], w_gu[j])
    y, z = meta[WHO] // 2, lax.rem(meta[WHO], 2)
    for k in range(NY):
        owner = 2 * lax.rem(y + k, NY)
        for e in range(SHARE):
            keep[k, e] = acc[(owner + z) * SHARE + e].astype(BF16)
            pass_on[k, e] = acc[(owner + 1 - z) * SHARE + e].astype(BF16)


def out_part_body(meta, hd, w_d, *rest):
    outs, acc = rest[:NY], rest[NY]
    acc[...] = jnp.zeros_like(acc)
    for j in range(LIVE):
        c = meta[D_COL + j]
        acc[c] = acc[c] + dot(hd[meta[D_SLOT + j]], w_d[j])
    for k in range(NY):
        owner = 2 * lax.rem(meta[WHO] // 2 + k, NY)
        for i in range(2):
            for e in range(SHARE):
                outs[k][i, e] = acc[(owner + i) * SHARE + e].astype(BF16)


def token_pair_body(keep, came, *outs):
    for k in range(NY):
        outs[k][...] = (keep[k].astype(F32) + came[k].astype(F32)).astype(BF16)


def out_y_body(meta, *refs):
    got, (keep, pass_on) = refs[:NY], refs[NY:]
    z = lax.rem(meta[WHO], 2)
    for out, i in ((pass_on, 1 - z), (keep, z)):
        for e in range(SHARE):
            total = got[0][i, e].astype(F32)
            for ref in got[1:]:
                total = total + ref[i, e].astype(F32)
            out[e] = total.astype(BF16)


def small_grads_body(meta, parts, tok_t, cot, perm2, latents, grad):
    total = parts[0].astype(F32)
    for i in range(1, NMP):
        total = total + parts[i].astype(F32)
    total = total.astype(BF16)
    latents[0] = total[:, :RANK]
    latents[1] = total[:, RANK:]
    who = meta[WHO]
    rows = pl.ds(pl.multiple_of((who % 4) * 32, 32), 32)
    pieces = [tok_t[2 * d + who // 4, rows, :] for d in range(NDP)]
    low = dot(jnp.concatenate(pieces, axis=0), total[:, :RANK]).reshape(NDP, 32, RANK)
    low = jnp.concatenate([low[:, :16], low[:, 16:]], axis=2)
    grad[:, :16, :] = low.astype(BF16)
    down_t = turned(total)[RANK:]
    pieces = [dot(down_t, cot[:, span(who * SHARE + e)]).astype(BF16) for e in range(SHARE)]
    rows = dot(perm2[...], jnp.concatenate(pieces, axis=0)).astype(BF16)
    grad[:, 16:, :] = rows.reshape(NDP, 16, BLK)


def share_sum(refs, e):
    total = refs[0][e].astype(F32)
    for ref in refs[1:]:
        total = total + ref[e].astype(F32)
    return total


def token_out_body(*refs):
    got, (latents, low_share, out) = refs[:NY], refs[NY:]
    latent = latents[0]
    for e in range(SHARE):
        low = low_share[e // 2]
        low = low[:, :RANK] if e % 2 == 0 else low[:, RANK:]
        out[:, e * BLK : (e + 1) * BLK] = (share_sum(got, e) + dot_t(latent, low)).astype(BF16)


def layer_out_body(keep, came, latents, dlout, out):
    latent = latents[1]
    for e in range(SHARE):
        low = dot(latent, dlout[e * RANK : (e + 1) * RANK])
        out[:, e * BLK : (e + 1) * BLK] = (share_sum((keep, came), e) + low).astype(BF16)


def final_body(up_count, down_count, who, got, gate_o, up_o, down_o, mid_o, tail, red):
    total = got[0].astype(F32)
    for i in range(1, 4):
        total = total + got[i].astype(F32)
    red[...] = total.astype(BF16)
    mine = who[0] * SLOTS
    zero = jnp.zeros((4, BLK), BF16)

    def put(out, counts, base):
        at = jnp.int32(base)
        for s in range(SLOTS):
            count = counts[mine + s]
            for k in range(DEPTH):
                out[s, k] = jnp.where(k < count, red[at], zero)
                at = at + (k < count).astype(I32)

    put(gate_o, up_count, GATE)
    put(up_o, up_count, UP)
    put(down_o, down_count, GRAD_A + DOWN)
    for s in range(SLOTS):
        mid_o[:, s * BLK : (s + 1) * BLK] = red[MID + s]
    for e in range(8):
        tail[e] = red[GRAD_A + DLIN + e]


def lookup(table_ids, positions):
    span_ids = jnp.arange(table_ids.shape[0], dtype=I32)
    return jnp.sum(jnp.where(positions[..., None] == span_ids, table_ids, 0), axis=-1)


def own_rows(table_ids, mine):
    return lax.dynamic_slice_in_dim(table_ids, mine * SLOTS, SLOTS, 0)


def inverse_of(order_ids):
    ids = jnp.arange(order_ids.shape[0], dtype=I32)
    return jnp.sum(jnp.where(order_ids[None, :] == ids[:, None], ids[None, :], 0), axis=1)


def send_table(owner, peer, rank, local_slot, mine):
    lanes = jnp.arange(NMP * CAP, dtype=I32)
    target = peer * CAP + rank
    matched = (owner[None, :] == mine) & (target[None, :] == lanes[:, None])
    return jnp.sum(jnp.where(matched, local_slot[None, :], 0), axis=1)


def live_table(count, keys):
    live = (jnp.arange(DEPTH, dtype=I32)[None, :] < count[:, None]).reshape(-1)
    ids = jnp.arange(SLOTS * DEPTH, dtype=I32)
    place = jnp.sum(jnp.where((ids[None, :] < ids[:, None]) & live[None, :], 1, 0), axis=1)
    hit = (jnp.arange(LIVE, dtype=I32)[:, None] == place[None, :]) & live[None, :]
    flat = keys.reshape(-1)
    of_key = jnp.sum(jnp.where(hit, flat[None, :], 0), axis=1)
    of_slot = jnp.sum(jnp.where(hit, (ids // DEPTH)[None, :], 0), axis=1)
    return of_key, of_slot, flat, jnp.where(live, place, LIVE)


def tables(mine, up_order, down_order, up_rows, down_cols, up_count, down_count):
    slot_ids = jnp.arange(up_order.shape[0], dtype=I32)
    source = lookup(inverse_of(up_order), down_order)
    from_device, to_device = source // SLOTS, slot_ids // SLOTS
    earlier = (
        (from_device[None, :] == from_device[:, None])
        & (to_device[None, :] == to_device[:, None])
        & (slot_ids[None, :] < slot_ids[:, None])
    )
    rank = jnp.sum(earlier.astype(I32), axis=1)
    send_a = send_table(from_device, to_device, rank, source % SLOTS, mine)
    got_a = own_rows(from_device * CAP + rank, mine)
    send_b = send_table(to_device, from_device, rank, slot_ids % SLOTS, mine)
    blocks_down = lookup(inverse_of(down_order), own_rows(up_order, mine))
    got_b = lookup(to_device * CAP + rank, blocks_down)
    u = live_table(own_rows(up_count, mine), own_rows(up_rows, mine))
    d = live_table(own_rows(down_count, mine), own_rows(down_cols, mine))
    fields = [
        (U_ROW, u[0]), (U_SLOT, u[1]), (D_COL, d[0]), (D_SLOT, d[1]), (U_KEY, u[2]), (D_KEY, d[2]),
        (U_POS, u[3]), (D_POS, d[3]), (SEND_A, send_a), (SEND_B, send_b), (GOT_A, got_a),
        (GOT_B, got_b), (WHO, mine.reshape(1)),
    ]
    ends = [start for start, _ in fields[1:]] + [META]
    padded = [jnp.pad(v, (0, end - start - v.shape[0])) for (start, v), end in zip(fields, ends)]
    return jnp.concatenate(padded)


def permutations():
    r = jnp.arange(512, dtype=I32)
    q, rest = r // 16, r % 16
    plain = q
    chain = (q % 4) * 8 + (q // 4 % 4) * 2 + q // 16
    give = (q % 4) * 8 + q // 4
    row4 = lambda d: (rest // 4) * BLK + 4 * d + rest % 4
    row2 = lambda d: (rest // 2) * RANK + 2 * d + rest % 2
    out = lambda src: (src[:, None] == r[None, :]).astype(BF16)
    into = lambda src: (src[None, :] == r[:, None]).astype(BF16)
    return (
        into(row4(plain)), into(row4(chain)), into(row2(chain)),
        out(row4(give)), out(row2(give)), out(row2(plain)),
    )


def spread(x, axis, n):
    return lax.all_to_all(jnp.broadcast_to(x[None], (n,) + x.shape), axis, 0, 0, tiled=True)


def gather_step(x, axis, n):
    x = spread(x, axis, n)
    return x.reshape((-1,) + x.shape[-2:])


def together(values):
    return lax.optimization_barrier(values)


def rotate(parts):
    moved = [
        lax.ppermute(parts[k], "y", [(i, (i + k) % NY) for i in range(NY)]) for k in range(1, NY)
    ]
    return [parts[0]] + moved


def double(x, axis, pairs, upper):
    came = lax.ppermute(x, axis, pairs)
    return jnp.concatenate([jnp.where(upper, came, x), jnp.where(upper, x, came)], axis=0)


def local(
    tokens, cotangent, gate_weight, up_weight, down_weight, low_in, low_mid, down_low_in,
    down_low_out, up_order, down_order, up_rows, down_cols, up_count, down_count,
):
    mine = lax.axis_index(MP).astype(I32)
    who = mine.reshape(1)
    mid_rows = low_mid.reshape(4, SLOTS, BLK).transpose(1, 0, 2)
    dlin_rows = jnp.pad(
        down_low_in.reshape(2, SLOTS, BLK).transpose(1, 0, 2).reshape(2 * SLOTS, BLK), ((0, 4), (0, 0))
    ).reshape(8, 4, BLK)
    low_rows = jnp.concatenate([low_in[:BLK], low_in[BLK:]], axis=1).reshape(32, 4, BLK)
    dlout_rows = down_low_out.reshape(2, SHARE, BLK).transpose(1, 0, 2).reshape(4, 4, BLK)
    first, second = call(
        pack_body, (shape(PACK_A, 4, BLK), shape(PACK_B, 4, BLK)),
        (gate_weight, up_weight, down_weight, mid_rows, low_rows, dlin_rows, dlout_rows),
        (up_count, down_count, who),
    )
    got_up = lax.all_gather(first.reshape(4 * PACK_A, BLK), DP)
    got_down = gather_step(second.reshape(1, 4 * PACK_B, BLK), "zh", 4)
    ids = (mine, up_order, down_order, up_rows, down_cols, up_count, down_count)
    got_down, ids = together((got_down, ids))
    got_down = gather_step(got_down, "x", 4)
    meta = tables(*ids)
    take, take_c, take2_c, give, give2, give2_plain = permutations()
    got_down, meta = together((got_down, meta))
    got_down = gather_step(got_down, "core", 2)
    tok_t = tokens.reshape(BLK, COLS, BLK).transpose(1, 2, 0)

    slots = shape(SLOTS, BLK, BLK)
    slots_scratch = pltpu.VMEM((SLOTS, BLK, BLK), BF16)
    parcel = shape(NMP, CAP, BLK, BLK)
    got_down, take, give, give2, give2_plain = together((got_down, take, give, give2, give2_plain))
    back_send, w_d, dlin, dlout = call(
        hidden_grad_body,
        (
            shape(NMP, BACK_ROWS, BLK), shape(LIVE + 1, BLK, BLK), shape(SLOTS, RANK, BLK),
            shape(512, BLK),
        ),
        (got_down, cotangent, take_c, take2_c), (meta,), (slots_scratch,),
    )
    back_send, tok_t = together((back_send, tok_t))
    back_got = lax.all_to_all(back_send, MP, 0, 0, tiled=True)

    send, act, w_gu, mid, lat, low_share = call(
        forward_body,
        (
            parcel, shape(SLOTS, BLK, 2 * BLK, dtype=F32), shape(LIVE + 1, BLK, 2 * BLK), slots,
            shape(BLK, RANK), shape(4, BLK, BLK),
        ),
        (got_up, tokens, take), (meta,), (slots_scratch,),
    )
    got = lax.all_to_all(send, MP, 0, 0, tiled=True)

    hbm = pl.BlockSpec(memory_space=pl.ANY)
    vmem = pl.BlockSpec(memory_space=pltpu.VMEM)
    smem = pl.BlockSpec(memory_space=pltpu.SMEM)
    grad_shape = shape(NDP, 4 * GRAD, BLK)
    grad, gu, part_up, back_latent = pl.pallas_call(
        up_grads_body,
        out_shape=(
            grad_shape, shape(SLOTS, BLK, 2 * BLK), shape(BLK, RANK, dtype=F32), shape(BLK, RANK),
        ),
        in_specs=[smem] + [vmem] * 6,
        out_specs=(hbm, vmem, vmem, vmem),
        scratch_shapes=[
            slots_scratch, pltpu.VMEM((NDP, 4 * GRAD_A, BLK), BF16), pltpu.SemaphoreType.DMA,
        ],
        compiler_params=pltpu.CompilerParams(vmem_limit_bytes=VMEM_LIMIT),
    )(meta, back_got, act, mid, lat, tok_t, give)
    grad, hd, part_down = pl.pallas_call(
        down_grads_body,
        out_shape=(grad_shape, slots, shape(BLK, RANK, dtype=F32)),
        in_specs=[smem] + [vmem] * 6 + [hbm],
        out_specs=(hbm, vmem, vmem),
        scratch_shapes=[
            slots_scratch, pltpu.VMEM((SLOTS, RANK, BLK), BF16),
            pltpu.VMEM((NDP, 4 * (GRAD - GRAD_A), BLK), BF16), pltpu.SemaphoreType.DMA,
        ],
        input_output_aliases={7: 0},
        compiler_params=pltpu.CompilerParams(vmem_limit_bytes=VMEM_LIMIT),
    )(meta, got, dlin, back_latent, cotangent, give, give2, grad)
    grad = lax.psum_scatter(
        grad.reshape(NDP * 4 * GRAD, BLK), ("x", "core"), scatter_dimension=0, tiled=True
    )
    part = jnp.concatenate([part_up, part_down], axis=1).astype(BF16)
    parts = spread(part, MP, NMP)
    acc = pltpu.VMEM((COLS, BLK, BLK), F32)
    token_part = call(
        token_part_body, (shape(NY, SHARE, BLK, BLK),) * 2, (gu, w_gu), (meta,), (acc,)
    )
    out_part = call(
        out_part_body, (shape(2, SHARE, BLK, BLK),) * NY, (hd, w_d), (meta,), (acc,)
    )
    parts, token_part, out_part = together((parts, token_part, out_part))
    latents, small = call(
        small_grads_body, (shape(2, BLK, RANK), shape(NDP, 32, BLK)),
        (parts, tok_t, cotangent, give2_plain), (meta,),
    )

    swap = [(0, 1), (1, 0)]
    token_came = lax.ppermute(token_part[1], "zl", swap)
    out_got = rotate(out_part)
    small = lax.all_to_all(small, DP, 0, 0, tiled=True)
    small = jnp.sum(small.astype(F32), axis=0).astype(BF16)
    small, grad, token_came, out_got = together((small, grad, token_came, out_got))
    grad = lax.all_to_all(grad.reshape(4, 4 * GRAD, BLK), "zh", 0, 0, tiled=True)
    half = shape(SHARE, BLK, BLK)
    token_got = rotate(call(token_pair_body, (half,) * NY, (token_part[0], token_came), ()))
    out_keep, out_give = call(out_y_body, (half,) * 2, out_got, (meta,))
    out_came = lax.ppermute(out_give, "zl", swap)
    low_g = small[:16]
    y, z = lax.axis_index("y"), lax.axis_index("zl")
    low_g = double(low_g, "zl", swap, z == 1)
    low_g = double(low_g, "y", [(0, 1), (1, 0), (2, 3), (3, 2)], y % 2 == 1)
    low_g = double(low_g, "y", [(0, 2), (2, 0), (1, 3), (3, 1)], y >= 2)
    low_g = low_g.reshape(NMP, 16, BLK)
    wide = shape(BLK, SHARE * BLK)
    token_grad = call(token_out_body, wide, (*token_got, latents, low_share), ())
    layer_out = call(layer_out_body, wide, (out_keep, out_came, latents, dlout), ())
    wide = shape(SLOTS, DEPTH, 4, BLK)
    gate_g, up_g, down_g, mid_g, tail = call(
        final_body, (wide, wide, wide, shape(4, SLOTS * BLK), shape(8, 4, BLK)),
        (grad.reshape(4, GRAD, 4, BLK),), (up_count, down_count, who),
        (pltpu.VMEM((GRAD, 4, BLK), BF16),),
    )
    dlin_g = tail.reshape(16, 2, BLK)[:SLOTS].transpose(1, 0, 2).reshape(2, SLOTS * BLK)
    low_g = jnp.concatenate([low_g[:, :, :RANK], low_g[:, :, RANK:]], axis=1)
    low_in_grad = low_g.reshape(2 * BLK, RANK)
    dlout_g = small[16:].reshape(SHARE, 2, BLK).transpose(1, 0, 2).reshape(2, SHARE * BLK)
    return layer_out, token_grad, gate_g, up_g, down_g, low_in_grad, mid_g, dlin_g, dlout_g


def solution(mesh):
    fine = Mesh(mesh.devices.reshape(4, 4, 2, 4, 2), DP + MP)
    rows, both, blocks = P(DP, None), P(DP, MP), P(MP, None, DP, None)
    in_specs = (rows, rows, blocks, blocks, blocks, rows, both, both, both) + (P(),) * 6
    out_specs = (both, both, blocks, blocks, blocks, rows, both, both, both)
    return jax.shard_map(local, mesh=fine, in_specs=in_specs, out_specs=out_specs, check_vma=False)
```

```python
import jax
import jax.numpy as jnp
from jax import lax
from jax.experimental import pallas as pl
from jax.experimental.pallas import tpu as pltpu
from jax.sharding import Mesh, PartitionSpec as P

F32 = jnp.float32
BF16 = jnp.bfloat16
I32 = jnp.int32
DP = ("zh", "x", "core")
MP = ("y", "zl")
NDP, NMP = 32, 8
SLOTS, DEPTH, BLK = 14, 5, 128
LIVE = 42
RANK = 64
COLS = 64
SHARE = COLS // NMP
CAP = 2
NY = 4
BACK_LOW = CAP * BLK
BACK_SUM = BACK_LOW + CAP * RANK
BACK_ROWS = BACK_SUM + BLK
VMEM_LIMIT = 58 * 2**20

GATE, MID, UP, LOWIN, PACK_A = 0, 42, 56, 100, 132
DOWN, DLIN, DLOUT, PACK_B = 0, 44, 52, 56
GRAD_A, GRAD = 100, 152

U_ROW, U_SLOT, D_COL, D_SLOT = 0, 48, 96, 144
U_KEY, D_KEY, U_POS, D_POS = 192, 264, 336, 408
SEND_A, SEND_B, GOT_A, GOT_B, WHO, META = 480, 496, 512, 528, 544, 560


def dot(a, b):
    return lax.dot_general(a, b, (((1,), (0,)), ((), ())), preferred_element_type=F32)


def dot_t(a, b):
    return lax.dot_general(a, b, (((1,), (1,)), ((), ())), preferred_element_type=F32)


def turned(a):
    return a.astype(F32).T.astype(BF16)


def span(start):
    return pl.ds(pl.multiple_of(start * BLK, BLK), BLK)


def call(body, out_shapes, operands, scalars, scratch=()):
    vmem = pl.BlockSpec(memory_space=pltpu.VMEM)
    smem = pl.BlockSpec(memory_space=pltpu.SMEM)
    return pl.pallas_call(
        body,
        out_shape=out_shapes,
        in_specs=[smem] * len(scalars) + [vmem] * len(operands),
        out_specs=jax.tree.map(lambda _: vmem, out_shapes),
        scratch_shapes=list(scratch),
        compiler_params=pltpu.CompilerParams(vmem_limit_bytes=VMEM_LIMIT),
    )(*scalars, *operands)


def shape(*dims, dtype=BF16):
    return jax.ShapeDtypeStruct(dims, dtype)


def pack_body(up_count, down_count, who, gate_w, up_w, down_w, mid, low, dlin, dlout, first, second):
    mine = who[0] * SLOTS
    for pad in (UP + 42, UP + 43):
        first[pad] = jnp.zeros((4, BLK), BF16)
    for pad in (DOWN + 42, DOWN + 43):
        second[pad] = jnp.zeros((4, BLK), BF16)

    def put(out, weight, counts, base):
        at = jnp.int32(base)
        for s in range(SLOTS):
            count = counts[mine + s]
            for k in range(DEPTH):
                out[at] = weight[s, k]
                at = at + (k < count).astype(I32)

    put(second, down_w, down_count, DOWN)
    put(first, gate_w, up_count, GATE)
    put(first, up_w, up_count, UP)
    for s in range(SLOTS):
        first[MID + s] = mid[s]
    for e in range(32):
        first[LOWIN + e] = low[e]
    for e in range(8):
        second[DLIN + e] = dlin[e]
    for e in range(4):
        second[DLOUT + e] = dlout[e]


def hidden_grad_body(meta, got, cot, perm, perm2, send, w_d, dlin, dlout, hgrad):
    def rows(block):
        return got[:, 4 * block : 4 * block + 16, :].reshape(512, BLK)

    for g in range(0, 11, 2):
        blocks = [DOWN + 4 * i for i in (g, g + 1) if i < 11]
        both = dot(perm[...], jnp.concatenate([rows(b) for b in blocks], axis=1)).astype(BF16)
        for half in range(len(blocks)):
            for jj in range(4):
                j = 4 * (g + half) + jj
                if j < LIVE:
                    w_d[j] = both[jj * BLK : (jj + 1) * BLK, half * BLK : (half + 1) * BLK]
    w_d[LIVE] = jnp.zeros((BLK, BLK), BF16)
    joined = jnp.concatenate([rows(DLIN), rows(DLIN + 4)], axis=1)
    both = dot(perm2[...], joined).astype(BF16)
    for t in range(SLOTS):
        dlin[t] = both[(t % 8) * RANK : (t % 8 + 1) * RANK, (t // 8) * BLK : (t // 8 + 1) * BLK]
    who = meta[WHO] * SHARE
    low = dot(perm2[...], rows(DLOUT)).astype(BF16)
    dlout[...] = low
    total = jnp.zeros((BLK, RANK), F32)
    for e in range(SHARE):
        total = total + dot_t(cot[:, span(who + e)], low[e * RANK : (e + 1) * RANK])
    total = jnp.concatenate([total, jnp.zeros_like(total)], axis=1).astype(BF16)
    for t in range(SLOTS):
        acc = jnp.zeros((BLK, BLK), F32)
        for k in range(DEPTH):
            p = DEPTH * t + k
            acc = acc + dot_t(cot[:, span(meta[D_KEY + p])], w_d[meta[D_POS + p]])
        hgrad[t] = acc.astype(BF16)
    for lane in range(NMP * CAP):
        peer, c = lane // CAP, lane % CAP
        t = meta[SEND_B + lane]
        send[peer, c * BLK : (c + 1) * BLK] = hgrad[t]
        send[peer, BACK_LOW + c * RANK : BACK_LOW + (c + 1) * RANK] = dlin[t]
    for peer in range(NMP):
        send[peer, BACK_SUM:] = total


def forward_body(meta, got, tok, perm, send, act, w_gu, mid, lat, low_share, hid):
    def rows(block):
        return got[:, 4 * block : 4 * block + 16, :].reshape(512, BLK)

    def pair(first, second):
        joined = jnp.concatenate([rows(first), rows(second)], axis=1)
        return dot(perm[...], joined).astype(BF16)

    for g in range(11):
        both = pair(GATE + 4 * g, UP + 4 * g)
        for jj in range(4):
            piece = both[jj * BLK : (jj + 1) * BLK]
            if 4 * g + jj < LIVE:
                w_gu[4 * g + jj] = piece
            else:
                mid[4 * g + jj - LIVE] = piece[:, :BLK]
    w_gu[LIVE] = jnp.zeros((BLK, 2 * BLK), BF16)
    for a, b in ((2, 6), (10, 10)):
        both = pair(MID + a, MID + b)
        for half, i in enumerate((a, b)[: 1 + (a != b)]):
            for jj in range(4):
                mid[i + jj] = both[jj * BLK : (jj + 1) * BLK, half * BLK : (half + 1) * BLK]

    acc0 = jnp.zeros((BLK, BLK), F32)
    acc1 = jnp.zeros((BLK, BLK), F32)
    for d in range(NDP):
        low = got[d, 4 * LOWIN : 4 * PACK_A, :]
        acc0 = acc0 + dot(tok[:, 2 * d * BLK : (2 * d + 1) * BLK], low)
        acc1 = acc1 + dot(tok[:, (2 * d + 1) * BLK : (2 * d + 2) * BLK], low)
    latent = (acc0[:, :RANK] + acc1[:, RANK:]).astype(BF16)
    lat[...] = latent
    for i in range(4):
        low_share[i] = got[4 * meta[WHO] + i, 4 * LOWIN : 4 * PACK_A, :]

    for s in range(SLOTS):
        acc = jnp.concatenate([dot(latent, mid[s, :RANK]), dot(latent, mid[s, RANK:])], axis=1)
        for k in range(DEPTH):
            p = DEPTH * s + k
            acc = acc + dot(tok[:, span(meta[U_KEY + p])], w_gu[meta[U_POS + p]])
        gate, up = acc[:, :BLK], acc[:, BLK:]
        sig = jax.nn.sigmoid(gate)
        active = gate * sig
        hid[s] = (active * up).astype(BF16)
        act[s, :, :BLK] = up * sig * (1.0 + gate * (1.0 - sig))
        act[s, :, BLK:] = active
    for lane in range(NMP * CAP):
        send[lane // CAP, lane % CAP] = hid[meta[SEND_A + lane]]


def up_grads_body(
    meta, got, act, mid, lat, tok_t, perm, grad, gu, part, back_latent, midg, full, sem
):
    latent = lat[...]
    total = got[0, BACK_SUM:].astype(F32)
    for i in range(1, NMP):
        total = total + got[i, BACK_SUM:].astype(F32)
    back = total[:, :RANK].astype(BF16)
    back_latent[...] = back
    latent_t = turned(jnp.concatenate([latent, latent], axis=1))[:RANK]
    lat_sum = jnp.zeros((BLK, RANK), F32)
    for s in range(SLOTS):
        lane = meta[GOT_B + s]
        peer, c = lane // CAP, lane % CAP
        block = got[peer, span(c), :].astype(F32)
        at = pl.multiple_of(BACK_LOW + c * RANK, RANK)
        flow = (block + dot(back, got[peer, pl.ds(at, RANK), :])).astype(BF16).astype(F32)
        gg = (flow * act[s, :, :BLK]).astype(BF16)
        ug = (flow * act[s, :, BLK:]).astype(BF16)
        both = jnp.concatenate([gg, ug], axis=1)
        gu[s] = both
        lat_sum = lat_sum + dot_t(gg, mid[s, :RANK]) + dot_t(ug, mid[s, RANK:])
        two = dot(latent_t, both).astype(BF16)
        midg[s] = jnp.concatenate([two[:, :BLK], two[:, BLK:]], axis=0)
    part[...] = lat_sum

    def store(block, rows):
        full[:, 4 * block : 4 * block + 16, :] = rows.reshape(NDP, 16, BLK)

    zero = jnp.zeros((BLK, BLK), BF16)
    for g in range(11):
        pieces = []
        for j in range(4 * g, 4 * g + 4):
            if j < LIVE:
                piece = dot(tok_t[meta[U_ROW + j]], gu[meta[U_SLOT + j]]).astype(BF16)
            else:
                piece = jnp.concatenate([midg[j - LIVE], zero], axis=1)
            pieces.append(piece)
        both = dot(perm[...], jnp.concatenate(pieces, axis=0)).astype(BF16)
        store(GATE + 4 * g, both[:, :BLK])
        store(UP + 4 * g, both[:, BLK:])
    for i in (2, 6, 10):
        rows = jnp.concatenate([midg[i + jj] for jj in range(4)], axis=0)
        store(MID + i, dot(perm[...], rows).astype(BF16))
    copy = pltpu.make_async_copy(full, grad.at[:, : 4 * GRAD_A, :], sem)
    copy.start()
    copy.wait()


def down_grads_body(
    meta, got, dlin, back_latent, cot, perm, perm2, start, grad, hd, part, hd_t, ding, full, sem
):
    back = back_latent[...]
    back_t = turned(jnp.concatenate([back, back], axis=1))[:RANK]
    down_sum = jnp.zeros((BLK, RANK), F32)
    for t in range(SLOTS):
        lane = meta[GOT_A + t]
        h = got[lane // CAP, lane % CAP]
        hd[t] = h
        hd_t[t] = turned(h)
        down_sum = down_sum + dot_t(h, dlin[t])
        ding[t] = dot(back_t, h).astype(BF16)
    part[...] = down_sum

    def store(block, rows):
        full[:, 4 * block : 4 * block + 16, :] = rows.reshape(NDP, 16, BLK)

    zero = jnp.zeros((BLK, BLK), BF16)

    def tile_of(g):
        pieces = []
        for j in range(4 * g, 4 * g + 4):
            if j < LIVE:
                cols = cot[:, span(meta[D_COL + j])]
                pieces.append(dot(hd_t[meta[D_SLOT + j]], cols).astype(BF16))
            else:
                pieces.append(zero)
        return jnp.concatenate(pieces, axis=0)

    for g in range(0, 11, 2):
        tiles = [i for i in (g, g + 1) if i < 11]
        both = dot(perm[...], jnp.concatenate([tile_of(i) for i in tiles], axis=1)).astype(BF16)
        for half, i in enumerate(tiles):
            store(DOWN + 4 * i, both[:, half * BLK : (half + 1) * BLK])
    none = jnp.zeros((RANK, BLK), BF16)
    left = jnp.concatenate([ding[t] for t in range(8)], axis=0)
    right = jnp.concatenate([ding[t] for t in range(8, SLOTS)] + [none, none], axis=0)
    both = dot(perm2[...], jnp.concatenate([left, right], axis=1)).astype(BF16)
    store(DLIN, both[:, :BLK])
    store(DLIN + 4, both[:, BLK:])
    copy = pltpu.make_async_copy(full, grad.at[:, 4 * GRAD_A :, :], sem)
    copy.start()
    copy.wait()


def token_part_body(meta, gu, w_gu, keep, pass_on, acc):
    acc[...] = jnp.zeros_like(acc)
    for j in range(LIVE):
        r = meta[U_ROW + j]
        acc[r] = acc[r] + dot_t(gu[meta[U_SLOT + j]], w_gu[j])
    y, z = meta[WHO] // 2, lax.rem(meta[WHO], 2)
    for k in range(NY):
        owner = 2 * lax.rem(y + k, NY)
        for e in range(SHARE):
            keep[k, e] = acc[(owner + z) * SHARE + e].astype(BF16)
            pass_on[k, e] = acc[(owner + 1 - z) * SHARE + e].astype(BF16)


def out_part_body(meta, hd, w_d, *rest):
    outs, acc = rest[:NY], rest[NY]
    acc[...] = jnp.zeros_like(acc)
    for j in range(LIVE):
        c = meta[D_COL + j]
        acc[c] = acc[c] + dot(hd[meta[D_SLOT + j]], w_d[j])
    for k in range(NY):
        owner = 2 * lax.rem(meta[WHO] // 2 + k, NY)
        for i in range(2):
            for e in range(SHARE):
                outs[k][i, e] = acc[(owner + i) * SHARE + e].astype(BF16)


def token_pair_body(keep, came, *outs):
    for k in range(NY):
        outs[k][...] = (keep[k].astype(F32) + came[k].astype(F32)).astype(BF16)


def out_y_body(meta, *refs):
    got, (keep, pass_on) = refs[:NY], refs[NY:]
    z = lax.rem(meta[WHO], 2)
    for out, i in ((pass_on, 1 - z), (keep, z)):
        for e in range(SHARE):
            total = got[0][i, e].astype(F32)
            for ref in got[1:]:
                total = total + ref[i, e].astype(F32)
            out[e] = total.astype(BF16)


def small_grads_body(meta, parts, tok_t, cot, perm2, latents, grad):
    total = parts[0].astype(F32)
    for i in range(1, NMP):
        total = total + parts[i].astype(F32)
    total = total.astype(BF16)
    latents[0] = total[:, :RANK]
    latents[1] = total[:, RANK:]
    who = meta[WHO]
    rows = pl.ds(pl.multiple_of((who % 4) * 32, 32), 32)
    order = [(q % 4) * 8 + q // 4 for q in range(NDP)]
    pieces = [tok_t[2 * d + who // 4, rows, :] for d in order]
    low = dot(jnp.concatenate(pieces, axis=0), total[:, :RANK]).reshape(NDP, 32, RANK)
    low = jnp.concatenate([low[:, :16], low[:, 16:]], axis=2)
    grad[:, :16, :] = low.astype(BF16)
    down_t = turned(total)[RANK:]
    pieces = [dot(down_t, cot[:, span(who * SHARE + e)]).astype(BF16) for e in range(SHARE)]
    rows = dot(perm2[...], jnp.concatenate(pieces, axis=0)).astype(BF16)
    grad[:, 16:, :] = rows.reshape(NDP, 16, BLK)


def share_sum(refs, e):
    total = refs[0][e].astype(F32)
    for ref in refs[1:]:
        total = total + ref[e].astype(F32)
    return total


def token_out_body(*refs):
    got, (latents, low_share, out) = refs[:NY], refs[NY:]
    latent = latents[0]
    for e in range(SHARE):
        low = low_share[e // 2]
        low = low[:, :RANK] if e % 2 == 0 else low[:, RANK:]
        out[:, e * BLK : (e + 1) * BLK] = (share_sum(got, e) + dot_t(latent, low)).astype(BF16)


def layer_out_body(keep, came, latents, dlout, out):
    latent = latents[1]
    for e in range(SHARE):
        low = dot(latent, dlout[e * RANK : (e + 1) * RANK])
        out[:, e * BLK : (e + 1) * BLK] = (share_sum((keep, came), e) + low).astype(BF16)


def final_body(up_count, down_count, who, got, gate_o, up_o, down_o, mid_o, tail, red):
    total = got[0, :GRAD].astype(F32)
    for i in range(1, 4):
        total = total + got[i, :GRAD].astype(F32)
    red[...] = total.astype(BF16)
    mine = who[0] * SLOTS
    zero = jnp.zeros((4, BLK), BF16)

    def put(out, counts, base):
        at = jnp.int32(base)
        for s in range(SLOTS):
            count = counts[mine + s]
            for k in range(DEPTH):
                out[s, k] = jnp.where(k < count, red[at], zero)
                at = at + (k < count).astype(I32)

    put(gate_o, up_count, GATE)
    put(up_o, up_count, UP)
    put(down_o, down_count, GRAD_A + DOWN)
    for s in range(SLOTS):
        mid_o[:, s * BLK : (s + 1) * BLK] = red[MID + s]
    for e in range(8):
        tail[e] = red[GRAD_A + DLIN + e]


def lookup(table_ids, positions):
    span_ids = jnp.arange(table_ids.shape[0], dtype=I32)
    return jnp.sum(jnp.where(positions[..., None] == span_ids, table_ids, 0), axis=-1)


def own_rows(table_ids, mine):
    return lax.dynamic_slice_in_dim(table_ids, mine * SLOTS, SLOTS, 0)


def inverse_of(order_ids):
    ids = jnp.arange(order_ids.shape[0], dtype=I32)
    return jnp.sum(jnp.where(order_ids[None, :] == ids[:, None], ids[None, :], 0), axis=1)


def send_table(owner, peer, rank, local_slot, mine):
    lanes = jnp.arange(NMP * CAP, dtype=I32)
    target = peer * CAP + rank
    matched = (owner[None, :] == mine) & (target[None, :] == lanes[:, None])
    return jnp.sum(jnp.where(matched, local_slot[None, :], 0), axis=1)


def live_table(count, keys):
    live = (jnp.arange(DEPTH, dtype=I32)[None, :] < count[:, None]).reshape(-1)
    ids = jnp.arange(SLOTS * DEPTH, dtype=I32)
    place = jnp.sum(jnp.where((ids[None, :] < ids[:, None]) & live[None, :], 1, 0), axis=1)
    hit = (jnp.arange(LIVE, dtype=I32)[:, None] == place[None, :]) & live[None, :]
    flat = keys.reshape(-1)
    of_key = jnp.sum(jnp.where(hit, flat[None, :], 0), axis=1)
    of_slot = jnp.sum(jnp.where(hit, (ids // DEPTH)[None, :], 0), axis=1)
    return of_key, of_slot, flat, jnp.where(live, place, LIVE)


def tables(mine, up_order, down_order, up_rows, down_cols, up_count, down_count):
    slot_ids = jnp.arange(up_order.shape[0], dtype=I32)
    source = lookup(inverse_of(up_order), down_order)
    from_device, to_device = source // SLOTS, slot_ids // SLOTS
    earlier = (
        (from_device[None, :] == from_device[:, None])
        & (to_device[None, :] == to_device[:, None])
        & (slot_ids[None, :] < slot_ids[:, None])
    )
    rank = jnp.sum(earlier.astype(I32), axis=1)
    send_a = send_table(from_device, to_device, rank, source % SLOTS, mine)
    got_a = own_rows(from_device * CAP + rank, mine)
    send_b = send_table(to_device, from_device, rank, slot_ids % SLOTS, mine)
    blocks_down = lookup(inverse_of(down_order), own_rows(up_order, mine))
    got_b = lookup(to_device * CAP + rank, blocks_down)
    u = live_table(own_rows(up_count, mine), own_rows(up_rows, mine))
    d = live_table(own_rows(down_count, mine), own_rows(down_cols, mine))
    fields = [
        (U_ROW, u[0]), (U_SLOT, u[1]), (D_COL, d[0]), (D_SLOT, d[1]), (U_KEY, u[2]), (D_KEY, d[2]),
        (U_POS, u[3]), (D_POS, d[3]), (SEND_A, send_a), (SEND_B, send_b), (GOT_A, got_a),
        (GOT_B, got_b), (WHO, mine.reshape(1)),
    ]
    ends = [start for start, _ in fields[1:]] + [META]
    padded = [jnp.pad(v, (0, end - start - v.shape[0])) for (start, v), end in zip(fields, ends)]
    return jnp.concatenate(padded)


def permutations():
    r = jnp.arange(512, dtype=I32)
    q, rest = r // 16, r % 16
    plain = q
    chain = (q % 4) * 8 + (q // 4 % 4) * 2 + q // 16
    give = (q % 4) * 8 + q // 4
    row4 = lambda d: (rest // 4) * BLK + 4 * d + rest % 4
    row2 = lambda d: (rest // 2) * RANK + 2 * d + rest % 2
    out = lambda src: (src[:, None] == r[None, :]).astype(BF16)
    into = lambda src: (src[None, :] == r[:, None]).astype(BF16)
    return (
        into(row4(plain)), into(row4(chain)), into(row2(chain)),
        out(row4(give)), out(row2(give)),
    )


def spread(x, axis, n):
    return lax.all_to_all(jnp.broadcast_to(x[None], (n,) + x.shape), axis, 0, 0, tiled=True)


def gather_step(x, axis, n):
    x = spread(x, axis, n)
    return x.reshape((-1,) + x.shape[-2:])


def together(values):
    return lax.optimization_barrier(values)


def rotate(parts):
    moved = [
        lax.ppermute(parts[k], "y", [(i, (i + k) % NY) for i in range(NY)]) for k in range(1, NY)
    ]
    return [parts[0]] + moved


def local(
    tokens, cotangent, gate_weight, up_weight, down_weight, low_in, low_mid, down_low_in,
    down_low_out, up_order, down_order, up_rows, down_cols, up_count, down_count,
):
    mine = lax.axis_index(MP).astype(I32)
    who = mine.reshape(1)
    mid_rows = low_mid.reshape(4, SLOTS, BLK).transpose(1, 0, 2)
    dlin_rows = jnp.pad(
        down_low_in.reshape(2, SLOTS, BLK).transpose(1, 0, 2).reshape(2 * SLOTS, BLK), ((0, 4), (0, 0))
    ).reshape(8, 4, BLK)
    low_rows = jnp.concatenate([low_in[:BLK], low_in[BLK:]], axis=1).reshape(32, 4, BLK)
    dlout_rows = down_low_out.reshape(2, SHARE, BLK).transpose(1, 0, 2).reshape(4, 4, BLK)
    first, second = call(
        pack_body, (shape(PACK_A, 4, BLK), shape(PACK_B, 4, BLK)),
        (gate_weight, up_weight, down_weight, mid_rows, low_rows, dlin_rows, dlout_rows),
        (up_count, down_count, who),
    )
    got_up = lax.all_gather(first.reshape(4 * PACK_A, BLK), DP)
    got_down = gather_step(second.reshape(1, 4 * PACK_B, BLK), "zh", 4)
    ids = (mine, up_order, down_order, up_rows, down_cols, up_count, down_count)
    got_down, ids = together((got_down, ids))
    got_down = gather_step(got_down, "x", 4)
    meta = tables(*ids)
    take, take_c, take2_c, give, give2 = permutations()
    got_down, meta = together((got_down, meta))
    got_down = gather_step(got_down, "core", 2)
    tok_t = tokens.reshape(BLK, COLS, BLK).transpose(1, 2, 0)

    slots = shape(SLOTS, BLK, BLK)
    slots_scratch = pltpu.VMEM((SLOTS, BLK, BLK), BF16)
    parcel = shape(NMP, CAP, BLK, BLK)
    got_down, take, give, give2 = together((got_down, take, give, give2))
    back_send, w_d, dlin, dlout = call(
        hidden_grad_body,
        (
            shape(NMP, BACK_ROWS, BLK), shape(LIVE + 1, BLK, BLK), shape(SLOTS, RANK, BLK),
            shape(512, BLK),
        ),
        (got_down, cotangent, take_c, take2_c), (meta,), (slots_scratch,),
    )
    back_send, tok_t = together((back_send, tok_t))
    back_got = lax.all_to_all(back_send, MP, 0, 0, tiled=True)

    send, act, w_gu, mid, lat, low_share = call(
        forward_body,
        (
            parcel, shape(SLOTS, BLK, 2 * BLK, dtype=F32), shape(LIVE + 1, BLK, 2 * BLK), slots,
            shape(BLK, RANK), shape(4, BLK, BLK),
        ),
        (got_up, tokens, take), (meta,), (slots_scratch,),
    )
    got = lax.all_to_all(send, MP, 0, 0, tiled=True)

    hbm = pl.BlockSpec(memory_space=pl.ANY)
    vmem = pl.BlockSpec(memory_space=pltpu.VMEM)
    smem = pl.BlockSpec(memory_space=pltpu.SMEM)
    grad_shape = shape(NDP, 4 * GRAD, BLK)
    grad, gu, part_up, back_latent = pl.pallas_call(
        up_grads_body,
        out_shape=(
            grad_shape, shape(SLOTS, BLK, 2 * BLK), shape(BLK, RANK, dtype=F32), shape(BLK, RANK),
        ),
        in_specs=[smem] + [vmem] * 6,
        out_specs=(hbm, vmem, vmem, vmem),
        scratch_shapes=[
            slots_scratch, pltpu.VMEM((NDP, 4 * GRAD_A, BLK), BF16), pltpu.SemaphoreType.DMA,
        ],
        compiler_params=pltpu.CompilerParams(vmem_limit_bytes=VMEM_LIMIT),
    )(meta, back_got, act, mid, lat, tok_t, give)
    grad, hd, part_down = pl.pallas_call(
        down_grads_body,
        out_shape=(grad_shape, slots, shape(BLK, RANK, dtype=F32)),
        in_specs=[smem] + [vmem] * 6 + [hbm],
        out_specs=(hbm, vmem, vmem),
        scratch_shapes=[
            slots_scratch, pltpu.VMEM((SLOTS, RANK, BLK), BF16),
            pltpu.VMEM((NDP, 4 * (GRAD - GRAD_A), BLK), BF16), pltpu.SemaphoreType.DMA,
        ],
        input_output_aliases={7: 0},
        compiler_params=pltpu.CompilerParams(vmem_limit_bytes=VMEM_LIMIT),
    )(meta, got, dlin, back_latent, cotangent, give, give2, grad)
    grad = lax.psum_scatter(
        grad.reshape(NDP * 4 * GRAD, BLK), ("x", "core"), scatter_dimension=0, tiled=True
    )
    part = jnp.concatenate([part_up, part_down], axis=1).astype(BF16)
    parts = spread(part, MP, NMP)
    acc = pltpu.VMEM((COLS, BLK, BLK), F32)
    token_part = call(
        token_part_body, (shape(NY, SHARE, BLK, BLK),) * 2, (gu, w_gu), (meta,), (acc,)
    )
    out_part = call(
        out_part_body, (shape(2, SHARE, BLK, BLK),) * NY, (hd, w_d), (meta,), (acc,)
    )
    parts, token_part, out_part = together((parts, token_part, out_part))
    latents, small = call(
        small_grads_body, (shape(2, BLK, RANK), shape(NDP, 32, BLK)),
        (parts, tok_t, cotangent, give2), (meta,),
    )

    swap = [(0, 1), (1, 0)]
    token_came = lax.ppermute(token_part[1], "zl", swap)
    out_got = rotate(out_part)
    small = lax.all_to_all(small.reshape(8, BLK, BLK), ("x", "core"), 0, 0, tiled=True)
    small = jnp.sum(small.astype(F32), axis=0).astype(BF16).reshape(4, 32, BLK)
    small, grad, token_came, out_got = together((small, grad, token_came, out_got))
    grad = jnp.concatenate([grad.reshape(4, 4 * GRAD, BLK), small], axis=1)
    grad = lax.all_to_all(grad, "zh", 0, 0, tiled=True)
    small = jnp.sum(grad[:, 4 * GRAD :].astype(F32), axis=0).astype(BF16)
    half = shape(SHARE, BLK, BLK)
    token_got = rotate(call(token_pair_body, (half,) * NY, (token_part[0], token_came), ()))
    out_keep, out_give = call(out_y_body, (half,) * 2, out_got, (meta,))
    out_came = lax.ppermute(out_give, "zl", swap)
    low_g = spread(small[:16], MP, NMP)
    wide = shape(BLK, SHARE * BLK)
    token_grad = call(token_out_body, wide, (*token_got, latents, low_share), ())
    layer_out = call(layer_out_body, wide, (out_keep, out_came, latents, dlout), ())
    wide = shape(SLOTS, DEPTH, 4, BLK)
    gate_g, up_g, down_g, mid_g, tail = call(
        final_body, (wide, wide, wide, shape(4, SLOTS * BLK), shape(8, 4, BLK)),
        (grad.reshape(4, GRAD + 8, 4, BLK),), (up_count, down_count, who),
        (pltpu.VMEM((GRAD, 4, BLK), BF16),),
    )
    dlin_g = tail.reshape(16, 2, BLK)[:SLOTS].transpose(1, 0, 2).reshape(2, SLOTS * BLK)
    low_g = jnp.concatenate([low_g[:, :, :RANK], low_g[:, :, RANK:]], axis=1)
    low_in_grad = low_g.reshape(2 * BLK, RANK)
    dlout_g = small[16:].reshape(SHARE, 2, BLK).transpose(1, 0, 2).reshape(2, SHARE * BLK)
    return layer_out, token_grad, gate_g, up_g, down_g, low_in_grad, mid_g, dlin_g, dlout_g


def solution(mesh):
    fine = Mesh(mesh.devices.reshape(4, 4, 2, 4, 2), DP + MP)
    rows, both, blocks = P(DP, None), P(DP, MP), P(MP, None, DP, None)
    in_specs = (rows, rows, blocks, blocks, blocks, rows, both, both, both) + (P(),) * 6
    out_specs = (both, both, blocks, blocks, blocks, rows, both, both, both)
    return jax.shard_map(local, mesh=fine, in_specs=in_specs, out_specs=out_specs, check_vma=False)
```

```python
import jax
import jax.numpy as jnp
from jax import lax
from jax.experimental import pallas as pl
from jax.experimental.pallas import tpu as pltpu
from jax.sharding import Mesh, PartitionSpec as P

F32 = jnp.float32
BF16 = jnp.bfloat16
I32 = jnp.int32
DP = ("zh", "x", "core")
MP = ("y", "zl")
NDP, NMP = 32, 8
SLOTS, DEPTH, BLK = 14, 5, 128
LIVE = 42
RANK = 64
COLS = 64
SHARE = COLS // NMP
CAP = 2
NY = 4
BACK_LOW = CAP * BLK
BACK_SUM = BACK_LOW + CAP * RANK
BACK_ROWS = BACK_SUM + BLK
VMEM_LIMIT = 58 * 2**20

GATE, MID, UP, LOWIN, PACK_A = 0, 42, 56, 100, 132
DOWN, DLIN, DLOUT, PACK_B = 0, 44, 52, 56
GRAD_A, GRAD = 100, 152

U_ROW, U_SLOT, D_COL, D_SLOT = 0, 48, 96, 144
U_KEY, D_KEY, U_POS, D_POS = 192, 264, 336, 408
SEND_A, SEND_B, GOT_A, GOT_B, WHO, META = 480, 496, 512, 528, 544, 560


def dot(a, b):
    return lax.dot_general(a, b, (((1,), (0,)), ((), ())), preferred_element_type=F32)


def dot_t(a, b):
    return lax.dot_general(a, b, (((1,), (1,)), ((), ())), preferred_element_type=F32)


def turned(a):
    return a.astype(F32).T.astype(BF16)


def span(start):
    return pl.ds(pl.multiple_of(start * BLK, BLK), BLK)


def call(body, out_shapes, operands, scalars, scratch=()):
    vmem = pl.BlockSpec(memory_space=pltpu.VMEM)
    smem = pl.BlockSpec(memory_space=pltpu.SMEM)
    return pl.pallas_call(
        body,
        out_shape=out_shapes,
        in_specs=[smem] * len(scalars) + [vmem] * len(operands),
        out_specs=jax.tree.map(lambda _: vmem, out_shapes),
        scratch_shapes=list(scratch),
        compiler_params=pltpu.CompilerParams(vmem_limit_bytes=VMEM_LIMIT),
    )(*scalars, *operands)


def shape(*dims, dtype=BF16):
    return jax.ShapeDtypeStruct(dims, dtype)


def put_live(out, weight, counts, mine, base):
    at = jnp.int32(base)
    for s in range(SLOTS):
        count = counts[mine + s]
        for k in range(DEPTH):
            out[at] = weight[s, k]
            at = at + (k < count).astype(I32)


def pack_up_body(up_count, who, gate_w, up_w, mid, low, out):
    mine = who[0] * SLOTS
    for pad in (UP + 42, UP + 43):
        out[pad] = jnp.zeros((4, BLK), BF16)
    put_live(out, gate_w, up_count, mine, GATE)
    put_live(out, up_w, up_count, mine, UP)
    for s in range(SLOTS):
        out[MID + s] = mid[:, s * BLK : (s + 1) * BLK]
    for e in range(32):
        out[LOWIN + e] = low[e]


def pack_down_body(down_count, who, down_w, dlin, dlout, out):
    for pad in (DOWN + 42, DOWN + 43):
        out[pad] = jnp.zeros((4, BLK), BF16)
    put_live(out, down_w, down_count, who[0] * SLOTS, DOWN)
    for e in range(8):
        out[DLIN + e] = dlin[e]
    for e in range(4):
        out[DLOUT + e] = dlout[e]


def hidden_grad_body(meta, got, cot, perm, perm2, send, w_d, dlin, dlout, hgrad):
    def rows(block):
        return got[:, 4 * block : 4 * block + 16, :].reshape(512, BLK)

    for g in range(0, 11, 2):
        blocks = [DOWN + 4 * i for i in (g, g + 1) if i < 11]
        both = dot(perm[...], jnp.concatenate([rows(b) for b in blocks], axis=1)).astype(BF16)
        for half in range(len(blocks)):
            for jj in range(4):
                j = 4 * (g + half) + jj
                if j < LIVE:
                    w_d[j] = both[jj * BLK : (jj + 1) * BLK, half * BLK : (half + 1) * BLK]
    w_d[LIVE] = jnp.zeros((BLK, BLK), BF16)
    joined = jnp.concatenate([rows(DLIN), rows(DLIN + 4)], axis=1)
    both = dot(perm2[...], joined).astype(BF16)
    for t in range(SLOTS):
        dlin[t] = both[(t % 8) * RANK : (t % 8 + 1) * RANK, (t // 8) * BLK : (t // 8 + 1) * BLK]
    who = meta[WHO] * SHARE
    low = dot(perm2[...], rows(DLOUT)).astype(BF16)
    dlout[...] = low
    total = jnp.zeros((BLK, RANK), F32)
    for e in range(SHARE):
        total = total + dot_t(cot[:, span(who + e)], low[e * RANK : (e + 1) * RANK])
    total = jnp.concatenate([total, jnp.zeros_like(total)], axis=1).astype(BF16)
    for t in range(SLOTS):
        acc = jnp.zeros((BLK, BLK), F32)
        for k in range(DEPTH):
            p = DEPTH * t + k
            acc = acc + dot_t(cot[:, span(meta[D_KEY + p])], w_d[meta[D_POS + p]])
        hgrad[t] = acc.astype(BF16)
    for lane in range(NMP * CAP):
        peer, c = lane // CAP, lane % CAP
        t = meta[SEND_B + lane]
        send[peer, c * BLK : (c + 1) * BLK] = hgrad[t]
        send[peer, BACK_LOW + c * RANK : BACK_LOW + (c + 1) * RANK] = dlin[t]
    for peer in range(NMP):
        send[peer, BACK_SUM:] = total


def forward_body(
    meta, got_far, tok_far, perm, send, act, w_far, mid, lat, low_share, hid, got, tok, w_gu, sems
):
    loads = [
        pltpu.make_async_copy(
            got_far.at[:, : 4 * LOWIN, :], got.at[:, : 4 * LOWIN, :], sems.at[0]
        ),
        pltpu.make_async_copy(
            got_far.at[:, 4 * LOWIN :, :], got.at[:, 4 * LOWIN :, :], sems.at[1]
        ),
        pltpu.make_async_copy(tok_far, tok, sems.at[2]),
    ]
    for load in loads:
        load.start()
    loads[0].wait()

    def rows(block):
        return got[:, 4 * block : 4 * block + 16, :].reshape(512, BLK)

    def pair(first, second):
        joined = jnp.concatenate([rows(first), rows(second)], axis=1)
        return dot(perm[...], joined).astype(BF16)

    for g in range(11):
        both = pair(GATE + 4 * g, UP + 4 * g)
        for jj in range(4):
            piece = both[jj * BLK : (jj + 1) * BLK]
            if 4 * g + jj < LIVE:
                w_gu[4 * g + jj] = piece
            else:
                mid[4 * g + jj - LIVE] = piece[:, :BLK]
    w_gu[LIVE] = jnp.zeros((BLK, 2 * BLK), BF16)
    for a, b in ((2, 6), (10, 10)):
        both = pair(MID + a, MID + b)
        for half, i in enumerate((a, b)[: 1 + (a != b)]):
            for jj in range(4):
                mid[i + jj] = both[jj * BLK : (jj + 1) * BLK, half * BLK : (half + 1) * BLK]
    keep = pltpu.make_async_copy(w_gu, w_far, sems.at[3])
    keep.start()
    loads[1].wait()
    loads[2].wait()

    acc0 = jnp.zeros((BLK, BLK), F32)
    acc1 = jnp.zeros((BLK, BLK), F32)
    for d in range(NDP):
        low = got[d, 4 * LOWIN : 4 * PACK_A, :]
        acc0 = acc0 + dot(tok[:, 2 * d * BLK : (2 * d + 1) * BLK], low)
        acc1 = acc1 + dot(tok[:, (2 * d + 1) * BLK : (2 * d + 2) * BLK], low)
    latent = (acc0[:, :RANK] + acc1[:, RANK:]).astype(BF16)
    lat[...] = latent
    for i in range(4):
        low_share[i] = got[4 * meta[WHO] + i, 4 * LOWIN : 4 * PACK_A, :]

    for s in range(SLOTS):
        acc = jnp.concatenate([dot(latent, mid[s, :RANK]), dot(latent, mid[s, RANK:])], axis=1)
        for k in range(DEPTH):
            p = DEPTH * s + k
            acc = acc + dot(tok[:, span(meta[U_KEY + p])], w_gu[meta[U_POS + p]])
        gate, up = acc[:, :BLK], acc[:, BLK:]
        sig = jax.nn.sigmoid(gate)
        active = gate * sig
        hid[s] = (active * up).astype(BF16)
        act[s, :, :BLK] = up * sig * (1.0 + gate * (1.0 - sig))
        act[s, :, BLK:] = active
    for lane in range(NMP * CAP):
        send[lane // CAP, lane % CAP] = hid[meta[SEND_A + lane]]
    keep.wait()


def up_grads_body(
    meta, got, act, mid, lat, tok_t, perm, grad, gu, part, back_latent, midg, full, sem
):
    latent = lat[...]
    total = got[0, BACK_SUM:].astype(F32)
    for i in range(1, NMP):
        total = total + got[i, BACK_SUM:].astype(F32)
    back = total[:, :RANK].astype(BF16)
    back_latent[...] = back
    latent_t = turned(jnp.concatenate([latent, latent], axis=1))[:RANK]
    lat_sum = jnp.zeros((BLK, RANK), F32)
    for s in range(SLOTS):
        lane = meta[GOT_B + s]
        peer, c = lane // CAP, lane % CAP
        block = got[peer, span(c), :].astype(F32)
        at = pl.multiple_of(BACK_LOW + c * RANK, RANK)
        flow = (block + dot(back, got[peer, pl.ds(at, RANK), :])).astype(BF16).astype(F32)
        gg = (flow * act[s, :, :BLK]).astype(BF16)
        ug = (flow * act[s, :, BLK:]).astype(BF16)
        both = jnp.concatenate([gg, ug], axis=1)
        gu[s] = both
        lat_sum = lat_sum + dot_t(gg, mid[s, :RANK]) + dot_t(ug, mid[s, RANK:])
        two = dot(latent_t, both).astype(BF16)
        midg[s] = jnp.concatenate([two[:, :BLK], two[:, BLK:]], axis=0)
    part[...] = lat_sum

    def store(block, rows):
        full[:, 4 * block : 4 * block + 16, :] = rows.reshape(NDP, 16, BLK)

    zero = jnp.zeros((BLK, BLK), BF16)
    for g in range(11):
        pieces = []
        for j in range(4 * g, 4 * g + 4):
            if j < LIVE:
                piece = dot(tok_t[meta[U_ROW + j]], gu[meta[U_SLOT + j]]).astype(BF16)
            else:
                piece = jnp.concatenate([midg[j - LIVE], zero], axis=1)
            pieces.append(piece)
        both = dot(perm[...], jnp.concatenate(pieces, axis=0)).astype(BF16)
        store(GATE + 4 * g, both[:, :BLK])
        store(UP + 4 * g, both[:, BLK:])
    for i in (2, 6, 10):
        rows = jnp.concatenate([midg[i + jj] for jj in range(4)], axis=0)
        store(MID + i, dot(perm[...], rows).astype(BF16))
    copy = pltpu.make_async_copy(full, grad.at[:, : 4 * GRAD_A, :], sem)
    copy.start()
    copy.wait()


def down_grads_body(
    meta, got, dlin, back_latent, cot_far, perm, perm2, start, grad, hd, part, hd_t, ding, full,
    cot, sem, cot_sem,
):
    load = pltpu.make_async_copy(cot_far, cot, cot_sem)
    load.start()
    back = back_latent[...]
    back_t = turned(jnp.concatenate([back, back], axis=1))[:RANK]
    down_sum = jnp.zeros((BLK, RANK), F32)
    for t in range(SLOTS):
        lane = meta[GOT_A + t]
        h = got[lane // CAP, lane % CAP]
        hd[t] = h
        hd_t[t] = turned(h)
        down_sum = down_sum + dot_t(h, dlin[t])
        ding[t] = dot(back_t, h).astype(BF16)
    part[...] = down_sum
    load.wait()

    def store(block, rows):
        full[:, 4 * block : 4 * block + 16, :] = rows.reshape(NDP, 16, BLK)

    zero = jnp.zeros((BLK, BLK), BF16)

    def tile_of(g):
        pieces = []
        for j in range(4 * g, 4 * g + 4):
            if j < LIVE:
                cols = cot[:, span(meta[D_COL + j])]
                pieces.append(dot(hd_t[meta[D_SLOT + j]], cols).astype(BF16))
            else:
                pieces.append(zero)
        return jnp.concatenate(pieces, axis=0)

    for g in range(0, 11, 2):
        tiles = [i for i in (g, g + 1) if i < 11]
        both = dot(perm[...], jnp.concatenate([tile_of(i) for i in tiles], axis=1)).astype(BF16)
        for half, i in enumerate(tiles):
            store(DOWN + 4 * i, both[:, half * BLK : (half + 1) * BLK])
    none = jnp.zeros((RANK, BLK), BF16)
    left = jnp.concatenate([ding[t] for t in range(8)], axis=0)
    right = jnp.concatenate([ding[t] for t in range(8, SLOTS)] + [none, none], axis=0)
    both = dot(perm2[...], jnp.concatenate([left, right], axis=1)).astype(BF16)
    store(DLIN, both[:, :BLK])
    store(DLIN + 4, both[:, BLK:])
    copy = pltpu.make_async_copy(full, grad.at[:, 4 * GRAD_A :, :], sem)
    copy.start()
    copy.wait()


def token_part_body(meta, gu, w_gu, keep, pass_on, acc):
    acc[...] = jnp.zeros_like(acc)
    for j in range(LIVE):
        r = meta[U_ROW + j]
        acc[r] = acc[r] + dot_t(gu[meta[U_SLOT + j]], w_gu[j])
    y, z = meta[WHO] // 2, lax.rem(meta[WHO], 2)
    for k in range(NY):
        owner = 2 * lax.rem(y + k, NY)
        for e in range(SHARE):
            keep[k, e] = acc[(owner + z) * SHARE + e].astype(BF16)
            pass_on[k, e] = acc[(owner + 1 - z) * SHARE + e].astype(BF16)


def out_part_body(meta, hd, w_d, *rest):
    outs, acc = rest[:NY], rest[NY]
    acc[...] = jnp.zeros_like(acc)
    for j in range(LIVE):
        c = meta[D_COL + j]
        acc[c] = acc[c] + dot(hd[meta[D_SLOT + j]], w_d[j])
    for k in range(NY):
        owner = 2 * lax.rem(meta[WHO] // 2 + k, NY)
        for i in range(2):
            for e in range(SHARE):
                outs[k][i, e] = acc[(owner + i) * SHARE + e].astype(BF16)


def token_pair_body(keep, came, *outs):
    for k in range(NY):
        outs[k][...] = (keep[k].astype(F32) + came[k].astype(F32)).astype(BF16)


def out_y_body(meta, *refs):
    got, (keep, pass_on) = refs[:NY], refs[NY:]
    z = lax.rem(meta[WHO], 2)
    for out, i in ((pass_on, 1 - z), (keep, z)):
        for e in range(SHARE):
            total = got[0][i, e].astype(F32)
            for ref in got[1:]:
                total = total + ref[i, e].astype(F32)
            out[e] = total.astype(BF16)


def small_grads_body(meta, parts, tok_t, cot, perm2, latents, grad):
    total = parts[0].astype(F32)
    for i in range(1, NMP):
        total = total + parts[i].astype(F32)
    total = total.astype(BF16)
    latents[0] = total[:, :RANK]
    latents[1] = total[:, RANK:]
    who = meta[WHO]
    rows = pl.ds(pl.multiple_of((who % 4) * 32, 32), 32)
    order = [(q % 4) * 8 + q // 4 for q in range(NDP)]
    pieces = [tok_t[2 * d + who // 4, rows, :] for d in order]
    low = dot(jnp.concatenate(pieces, axis=0), total[:, :RANK]).reshape(NDP, 32, RANK)
    low = jnp.concatenate([low[:, :16], low[:, 16:]], axis=2)
    grad[:, :16, :] = low.astype(BF16)
    down_t = turned(total)[RANK:]
    pieces = [dot(down_t, cot[:, span(who * SHARE + e)]).astype(BF16) for e in range(SHARE)]
    rows = dot(perm2[...], jnp.concatenate(pieces, axis=0)).astype(BF16)
    grad[:, 16:, :] = rows.reshape(NDP, 16, BLK)


def share_sum(refs, e):
    total = refs[0][e].astype(F32)
    for ref in refs[1:]:
        total = total + ref[e].astype(F32)
    return total


def token_out_body(*refs):
    got, (latents, low_share, out) = refs[:NY], refs[NY:]
    latent = latents[0]
    for e in range(SHARE):
        low = low_share[e // 2]
        low = low[:, :RANK] if e % 2 == 0 else low[:, RANK:]
        out[:, e * BLK : (e + 1) * BLK] = (share_sum(got, e) + dot_t(latent, low)).astype(BF16)


def layer_out_body(keep, came, latents, dlout, out):
    latent = latents[1]
    for e in range(SHARE):
        low = dot(latent, dlout[e * RANK : (e + 1) * RANK])
        out[:, e * BLK : (e + 1) * BLK] = (share_sum((keep, came), e) + low).astype(BF16)


def final_body(up_count, down_count, who, got, gate_o, up_o, down_o, mid_o, tail, red):
    total = got[0, :GRAD].astype(F32)
    for i in range(1, 4):
        total = total + got[i, :GRAD].astype(F32)
    red[...] = total.astype(BF16)
    mine = who[0] * SLOTS
    zero = jnp.zeros((4, BLK), BF16)

    def put(out, counts, base):
        at = jnp.int32(base)
        for s in range(SLOTS):
            count = counts[mine + s]
            for k in range(DEPTH):
                out[s, k] = jnp.where(k < count, red[at], zero)
                at = at + (k < count).astype(I32)

    put(gate_o, up_count, GATE)
    put(up_o, up_count, UP)
    put(down_o, down_count, GRAD_A + DOWN)
    for s in range(SLOTS):
        mid_o[:, s * BLK : (s + 1) * BLK] = red[MID + s]
    for e in range(8):
        tail[e] = red[GRAD_A + DLIN + e]


def lookup(table_ids, positions):
    span_ids = jnp.arange(table_ids.shape[0], dtype=I32)
    return jnp.sum(jnp.where(positions[..., None] == span_ids, table_ids, 0), axis=-1)


def own_rows(table_ids, mine):
    return lax.dynamic_slice_in_dim(table_ids, mine * SLOTS, SLOTS, 0)


def inverse_of(order_ids):
    ids = jnp.arange(order_ids.shape[0], dtype=I32)
    return jnp.sum(jnp.where(order_ids[None, :] == ids[:, None], ids[None, :], 0), axis=1)


def send_table(owner, peer, rank, local_slot, mine):
    lanes = jnp.arange(NMP * CAP, dtype=I32)
    target = peer * CAP + rank
    matched = (owner[None, :] == mine) & (target[None, :] == lanes[:, None])
    return jnp.sum(jnp.where(matched, local_slot[None, :], 0), axis=1)


def live_table(count, keys):
    live = (jnp.arange(DEPTH, dtype=I32)[None, :] < count[:, None]).reshape(-1)
    ids = jnp.arange(SLOTS * DEPTH, dtype=I32)
    place = jnp.sum(jnp.where((ids[None, :] < ids[:, None]) & live[None, :], 1, 0), axis=1)
    hit = (jnp.arange(LIVE, dtype=I32)[:, None] == place[None, :]) & live[None, :]
    flat = keys.reshape(-1)
    of_key = jnp.sum(jnp.where(hit, flat[None, :], 0), axis=1)
    of_slot = jnp.sum(jnp.where(hit, (ids // DEPTH)[None, :], 0), axis=1)
    return of_key, of_slot, flat, jnp.where(live, place, LIVE)


def tables(mine, up_order, down_order, up_rows, down_cols, up_count, down_count):
    slot_ids = jnp.arange(up_order.shape[0], dtype=I32)
    source = lookup(inverse_of(up_order), down_order)
    from_device, to_device = source // SLOTS, slot_ids // SLOTS
    earlier = (
        (from_device[None, :] == from_device[:, None])
        & (to_device[None, :] == to_device[:, None])
        & (slot_ids[None, :] < slot_ids[:, None])
    )
    rank = jnp.sum(earlier.astype(I32), axis=1)
    send_a = send_table(from_device, to_device, rank, source % SLOTS, mine)
    got_a = own_rows(from_device * CAP + rank, mine)
    send_b = send_table(to_device, from_device, rank, slot_ids % SLOTS, mine)
    blocks_down = lookup(inverse_of(down_order), own_rows(up_order, mine))
    got_b = lookup(to_device * CAP + rank, blocks_down)
    u = live_table(own_rows(up_count, mine), own_rows(up_rows, mine))
    d = live_table(own_rows(down_count, mine), own_rows(down_cols, mine))
    fields = [
        (U_ROW, u[0]), (U_SLOT, u[1]), (D_COL, d[0]), (D_SLOT, d[1]), (U_KEY, u[2]), (D_KEY, d[2]),
        (U_POS, u[3]), (D_POS, d[3]), (SEND_A, send_a), (SEND_B, send_b), (GOT_A, got_a),
        (GOT_B, got_b), (WHO, mine.reshape(1)),
    ]
    ends = [start for start, _ in fields[1:]] + [META]
    padded = [jnp.pad(v, (0, end - start - v.shape[0])) for (start, v), end in zip(fields, ends)]
    return jnp.concatenate(padded)


def permutations():
    r = jnp.arange(512, dtype=I32)
    q, rest = r // 16, r % 16
    plain = q
    chain = (q % 4) * 8 + (q // 4 % 4) * 2 + q // 16
    give = (q % 4) * 8 + q // 4
    row4 = lambda d: (rest // 4) * BLK + 4 * d + rest % 4
    row2 = lambda d: (rest // 2) * RANK + 2 * d + rest % 2
    out = lambda src: (src[:, None] == r[None, :]).astype(BF16)
    into = lambda src: (src[None, :] == r[:, None]).astype(BF16)
    return (
        into(row4(plain)), into(row4(chain)), into(row2(chain)),
        out(row4(give)), out(row2(give)),
    )


def spread(x, axis, n):
    return lax.all_to_all(jnp.broadcast_to(x[None], (n,) + x.shape), axis, 0, 0, tiled=True)


def gather_step(x, axis, n):
    x = spread(x, axis, n)
    return x.reshape((-1,) + x.shape[-2:])


def together(values):
    return lax.optimization_barrier(values)


def rotate(parts):
    moved = [
        lax.ppermute(parts[k], "y", [(i, (i + k) % NY) for i in range(NY)]) for k in range(1, NY)
    ]
    return [parts[0]] + moved


def local(
    tokens, cotangent, gate_weight, up_weight, down_weight, low_in, low_mid, down_low_in,
    down_low_out, up_order, down_order, up_rows, down_cols, up_count, down_count,
):
    mine = lax.axis_index(MP).astype(I32)
    who = mine.reshape(1)
    low_rows = jnp.concatenate([low_in[:BLK], low_in[BLK:]], axis=1).reshape(32, 4, BLK)
    first = call(
        pack_up_body, shape(PACK_A, 4, BLK), (gate_weight, up_weight, low_mid, low_rows),
        (up_count, who),
    )
    first, down_low_in, down_low_out = together((first, down_low_in, down_low_out))
    dlin_rows = jnp.pad(
        down_low_in.reshape(2, SLOTS, BLK).transpose(1, 0, 2).reshape(2 * SLOTS, BLK), ((0, 4), (0, 0))
    ).reshape(8, 4, BLK)
    dlout_rows = down_low_out.reshape(2, SHARE, BLK).transpose(1, 0, 2).reshape(4, 4, BLK)
    second = call(
        pack_down_body, shape(PACK_B, 4, BLK), (down_weight, dlin_rows, dlout_rows),
        (down_count, who),
    )
    got_up = lax.all_gather(first.reshape(4 * PACK_A, BLK), DP)
    got_down = gather_step(second.reshape(1, 4 * PACK_B, BLK), "zh", 4)
    ids = (mine, up_order, down_order, up_rows, down_cols, up_count, down_count)
    got_down, ids = together((got_down, ids))
    got_down = gather_step(got_down, "x", 4)
    meta = tables(*ids)
    take, take_c, take2_c, give, give2 = permutations()
    got_down, meta = together((got_down, meta))
    got_down = gather_step(got_down, "core", 2)
    tok_t = tokens.reshape(BLK, COLS, BLK).transpose(1, 2, 0)

    slots = shape(SLOTS, BLK, BLK)
    slots_scratch = pltpu.VMEM((SLOTS, BLK, BLK), BF16)
    parcel = shape(NMP, CAP, BLK, BLK)
    got_down, take, give, give2 = together((got_down, take, give, give2))
    back_send, w_d, dlin, dlout = call(
        hidden_grad_body,
        (
            shape(NMP, BACK_ROWS, BLK), shape(LIVE + 1, BLK, BLK), shape(SLOTS, RANK, BLK),
            shape(512, BLK),
        ),
        (got_down, cotangent, take_c, take2_c), (meta,), (slots_scratch,),
    )
    back_send, tok_t = together((back_send, tok_t))
    back_got = lax.all_to_all(back_send, MP, 0, 0, tiled=True)

    hbm = pl.BlockSpec(memory_space=pl.ANY)
    vmem = pl.BlockSpec(memory_space=pltpu.VMEM)
    smem = pl.BlockSpec(memory_space=pltpu.SMEM)
    weights = (LIVE + 1, BLK, 2 * BLK)
    send, act, w_gu, mid, lat, low_share = pl.pallas_call(
        forward_body,
        out_shape=(
            parcel, shape(SLOTS, BLK, 2 * BLK, dtype=F32), shape(*weights), slots,
            shape(BLK, RANK), shape(4, BLK, BLK),
        ),
        in_specs=[smem, hbm, hbm, vmem],
        out_specs=(vmem, vmem, hbm, vmem, vmem, vmem),
        scratch_shapes=[
            slots_scratch, pltpu.VMEM((NDP, 4 * PACK_A, BLK), BF16),
            pltpu.VMEM((BLK, COLS * BLK), BF16), pltpu.VMEM(weights, BF16),
            pltpu.SemaphoreType.DMA((4,)),
        ],
        compiler_params=pltpu.CompilerParams(vmem_limit_bytes=VMEM_LIMIT),
    )(meta, got_up, tokens, take)
    got = lax.all_to_all(send, MP, 0, 0, tiled=True)

    grad_shape = shape(NDP, 4 * GRAD, BLK)
    grad, gu, part_up, back_latent = pl.pallas_call(
        up_grads_body,
        out_shape=(
            grad_shape, shape(SLOTS, BLK, 2 * BLK), shape(BLK, RANK, dtype=F32), shape(BLK, RANK),
        ),
        in_specs=[smem] + [vmem] * 6,
        out_specs=(hbm, vmem, vmem, vmem),
        scratch_shapes=[
            slots_scratch, pltpu.VMEM((NDP, 4 * GRAD_A, BLK), BF16), pltpu.SemaphoreType.DMA,
        ],
        compiler_params=pltpu.CompilerParams(vmem_limit_bytes=VMEM_LIMIT),
    )(meta, back_got, act, mid, lat, tok_t, give)
    grad, hd, part_down = pl.pallas_call(
        down_grads_body,
        out_shape=(grad_shape, slots, shape(BLK, RANK, dtype=F32)),
        in_specs=[smem] + [vmem] * 3 + [hbm] + [vmem] * 2 + [hbm],
        out_specs=(hbm, vmem, vmem),
        scratch_shapes=[
            slots_scratch, pltpu.VMEM((SLOTS, RANK, BLK), BF16),
            pltpu.VMEM((NDP, 4 * (GRAD - GRAD_A), BLK), BF16),
            pltpu.VMEM((BLK, COLS * BLK), BF16), pltpu.SemaphoreType.DMA, pltpu.SemaphoreType.DMA,
        ],
        input_output_aliases={7: 0},
        compiler_params=pltpu.CompilerParams(vmem_limit_bytes=VMEM_LIMIT),
    )(meta, got, dlin, back_latent, cotangent, give, give2, grad)
    grad = lax.psum_scatter(
        grad.reshape(NDP * 4 * GRAD, BLK), ("x", "core"), scatter_dimension=0, tiled=True
    )
    part = jnp.concatenate([part_up, part_down], axis=1).astype(BF16)
    parts = spread(part, MP, NMP)
    acc = pltpu.VMEM((COLS, BLK, BLK), F32)
    token_part = call(
        token_part_body, (shape(NY, SHARE, BLK, BLK),) * 2, (gu, w_gu), (meta,), (acc,)
    )
    out_part = call(
        out_part_body, (shape(2, SHARE, BLK, BLK),) * NY, (hd, w_d), (meta,), (acc,)
    )
    parts, token_part, out_part = together((parts, token_part, out_part))
    latents, small = call(
        small_grads_body, (shape(2, BLK, RANK), shape(NDP, 32, BLK)),
        (parts, tok_t, cotangent, give2), (meta,),
    )

    swap = [(0, 1), (1, 0)]
    token_came = lax.ppermute(token_part[1], "zl", swap)
    out_got = rotate(out_part)
    small = lax.all_to_all(small.reshape(8, BLK, BLK), ("x", "core"), 0, 0, tiled=True)
    small = jnp.sum(small.astype(F32), axis=0).astype(BF16).reshape(4, 32, BLK)
    small, grad, token_came, out_got = together((small, grad, token_came, out_got))
    grad = jnp.concatenate([grad.reshape(4, 4 * GRAD, BLK), small], axis=1)
    grad = lax.all_to_all(grad, "zh", 0, 0, tiled=True)
    half = shape(SHARE, BLK, BLK)
    token_got = rotate(call(token_pair_body, (half,) * NY, (token_part[0], token_came), ()))
    out_keep, out_give = call(out_y_body, (half,) * 2, out_got, (meta,))
    out_came = lax.ppermute(out_give, "zl", swap)
    wide = shape(BLK, SHARE * BLK)
    token_grad = call(token_out_body, wide, (*token_got, latents, low_share), ())
    grad, token_grad = together((grad, token_grad))
    small = jnp.sum(grad[:, 4 * GRAD :].astype(F32), axis=0).astype(BF16)
    low_g = spread(small[:16], MP, NMP)
    layer_out = call(layer_out_body, wide, (out_keep, out_came, latents, dlout), ())
    wide = shape(SLOTS, DEPTH, 4, BLK)
    gate_g, up_g, down_g, mid_g, tail = call(
        final_body, (wide, wide, wide, shape(4, SLOTS * BLK), shape(8, 4, BLK)),
        (grad.reshape(4, GRAD + 8, 4, BLK),), (up_count, down_count, who),
        (pltpu.VMEM((GRAD, 4, BLK), BF16),),
    )
    dlin_g = tail.reshape(16, 2, BLK)[:SLOTS].transpose(1, 0, 2).reshape(2, SLOTS * BLK)
    low_g = jnp.concatenate([low_g[:, :, :RANK], low_g[:, :, RANK:]], axis=1)
    low_in_grad = low_g.reshape(2 * BLK, RANK)
    dlout_g = small[16:].reshape(SHARE, 2, BLK).transpose(1, 0, 2).reshape(2, SHARE * BLK)
    return layer_out, token_grad, gate_g, up_g, down_g, low_in_grad, mid_g, dlin_g, dlout_g


def solution(mesh):
    fine = Mesh(mesh.devices.reshape(4, 4, 2, 4, 2), DP + MP)
    rows, both, blocks = P(DP, None), P(DP, MP), P(MP, None, DP, None)
    in_specs = (rows, rows, blocks, blocks, blocks, rows, both, both, both) + (P(),) * 6
    out_specs = (both, both, blocks, blocks, blocks, rows, both, both, both)
    return jax.shard_map(local, mesh=fine, in_specs=in_specs, out_specs=out_specs, check_vma=False)
```

```python
import jax
import jax.numpy as jnp
from jax import lax
from jax.experimental import pallas as pl
from jax.experimental.pallas import tpu as pltpu
from jax.sharding import Mesh, PartitionSpec as P

F32 = jnp.float32
BF16 = jnp.bfloat16
I32 = jnp.int32
DP = ("zh", "x", "core")
MP = ("y", "zl")
NDP, NMP = 32, 8
SLOTS, DEPTH, BLK = 14, 5, 128
LIVE = 42
RANK = 64
COLS = 64
SHARE = COLS // NMP
CAP = 2
NY = 4
BACK_LOW = CAP * BLK
BACK_SUM = BACK_LOW + CAP * RANK
BACK_ROWS = BACK_SUM + BLK
VMEM_LIMIT = 58 * 2**20

GATE, MID, UP, LOWIN, PACK_A = 0, 42, 56, 100, 132
DOWN, DLIN, DLOUT, PACK_B = 0, 44, 52, 56
GRAD_A, GRAD = 100, 152

U_ROW, U_SLOT, D_COL, D_SLOT = 0, 48, 96, 144
U_KEY, D_KEY, U_POS, D_POS = 192, 264, 336, 408
SEND_A, SEND_B, GOT_A, GOT_B, WHO, META = 480, 496, 512, 528, 544, 560


def dot(a, b):
    return lax.dot_general(a, b, (((1,), (0,)), ((), ())), preferred_element_type=F32)


def dot_t(a, b):
    return lax.dot_general(a, b, (((1,), (1,)), ((), ())), preferred_element_type=F32)


def turned(a):
    return a.astype(F32).T.astype(BF16)


def span(start):
    return pl.ds(pl.multiple_of(start * BLK, BLK), BLK)


def call(body, out_shapes, operands, scalars, scratch=()):
    vmem = pl.BlockSpec(memory_space=pltpu.VMEM)
    smem = pl.BlockSpec(memory_space=pltpu.SMEM)
    return pl.pallas_call(
        body,
        out_shape=out_shapes,
        in_specs=[smem] * len(scalars) + [vmem] * len(operands),
        out_specs=jax.tree.map(lambda _: vmem, out_shapes),
        scratch_shapes=list(scratch),
        compiler_params=pltpu.CompilerParams(vmem_limit_bytes=VMEM_LIMIT),
    )(*scalars, *operands)


def shape(*dims, dtype=BF16):
    return jax.ShapeDtypeStruct(dims, dtype)


def put_live(out, weight, counts, mine, base):
    at = jnp.int32(base)
    for s in range(SLOTS):
        count = counts[mine + s]
        for k in range(DEPTH):
            out[at] = weight[s, k]
            at = at + (k < count).astype(I32)


def pack_up_body(up_count, who, gate_w, up_w, mid, low, out):
    mine = who[0] * SLOTS
    for pad in (UP + 42, UP + 43):
        out[pad] = jnp.zeros((4, BLK), BF16)
    put_live(out, gate_w, up_count, mine, GATE)
    put_live(out, up_w, up_count, mine, UP)
    for s in range(SLOTS):
        out[MID + s] = mid[:, s * BLK : (s + 1) * BLK]
    for e in range(32):
        out[LOWIN + e] = low[e]


def pack_down_body(down_count, who, down_w, dlin, dlout, out):
    for pad in (DOWN + 42, DOWN + 43):
        out[pad] = jnp.zeros((4, BLK), BF16)
    put_live(out, down_w, down_count, who[0] * SLOTS, DOWN)
    for e in range(8):
        out[DLIN + e] = dlin[e]
    for e in range(4):
        out[DLOUT + e] = dlout[e]


def hidden_grad_body(meta, got, cot, perm, perm2, send, w_d, dlin, dlout, hgrad):
    def rows(block):
        return got[:, 4 * block : 4 * block + 16, :].reshape(512, BLK)

    for g in range(0, 11, 2):
        blocks = [DOWN + 4 * i for i in (g, g + 1) if i < 11]
        both = dot(perm[...], jnp.concatenate([rows(b) for b in blocks], axis=1)).astype(BF16)
        for half in range(len(blocks)):
            for jj in range(4):
                j = 4 * (g + half) + jj
                if j < LIVE:
                    w_d[j] = both[jj * BLK : (jj + 1) * BLK, half * BLK : (half + 1) * BLK]
    w_d[LIVE] = jnp.zeros((BLK, BLK), BF16)
    joined = jnp.concatenate([rows(DLIN), rows(DLIN + 4)], axis=1)
    both = dot(perm2[...], joined).astype(BF16)
    for t in range(SLOTS):
        dlin[t] = both[(t % 8) * RANK : (t % 8 + 1) * RANK, (t // 8) * BLK : (t // 8 + 1) * BLK]
    who = meta[WHO] * SHARE
    low = dot(perm2[...], rows(DLOUT)).astype(BF16)
    dlout[...] = low
    total = jnp.zeros((BLK, RANK), F32)
    for e in range(SHARE):
        total = total + dot_t(cot[:, span(who + e)], low[e * RANK : (e + 1) * RANK])
    total = jnp.concatenate([total, jnp.zeros_like(total)], axis=1).astype(BF16)
    for t in range(SLOTS):
        acc = jnp.zeros((BLK, BLK), F32)
        for k in range(DEPTH):
            p = DEPTH * t + k
            acc = acc + dot_t(cot[:, span(meta[D_KEY + p])], w_d[meta[D_POS + p]])
        hgrad[t] = acc.astype(BF16)
    for lane in range(NMP * CAP):
        peer, c = lane // CAP, lane % CAP
        t = meta[SEND_B + lane]
        send[peer, c * BLK : (c + 1) * BLK] = hgrad[t]
        send[peer, BACK_LOW + c * RANK : BACK_LOW + (c + 1) * RANK] = dlin[t]
    for peer in range(NMP):
        send[peer, BACK_SUM:] = total


def forward_body(
    meta, got_far, tok_far, perm, send, act, w_far, mid, lat, low_share, hid, got, tok, w_gu, sems
):
    loads = [
        pltpu.make_async_copy(
            got_far.at[:, : 4 * LOWIN, :], got.at[:, : 4 * LOWIN, :], sems.at[0]
        ),
        pltpu.make_async_copy(
            got_far.at[:, 4 * LOWIN :, :], got.at[:, 4 * LOWIN :, :], sems.at[1]
        ),
        pltpu.make_async_copy(tok_far, tok, sems.at[2]),
    ]
    for load in loads:
        load.start()
    loads[0].wait()

    def rows(block):
        return got[:, 4 * block : 4 * block + 16, :].reshape(512, BLK)

    def pair(first, second):
        joined = jnp.concatenate([rows(first), rows(second)], axis=1)
        return dot(perm[...], joined).astype(BF16)

    for g in range(11):
        both = pair(GATE + 4 * g, UP + 4 * g)
        for jj in range(4):
            piece = both[jj * BLK : (jj + 1) * BLK]
            if 4 * g + jj < LIVE:
                w_gu[4 * g + jj] = piece
            else:
                mid[4 * g + jj - LIVE] = piece[:, :BLK]
    w_gu[LIVE] = jnp.zeros((BLK, 2 * BLK), BF16)
    for a, b in ((2, 6), (10, 10)):
        both = pair(MID + a, MID + b)
        for half, i in enumerate((a, b)[: 1 + (a != b)]):
            for jj in range(4):
                mid[i + jj] = both[jj * BLK : (jj + 1) * BLK, half * BLK : (half + 1) * BLK]
    keep = pltpu.make_async_copy(w_gu, w_far, sems.at[3])
    keep.start()
    loads[1].wait()
    loads[2].wait()

    acc0 = jnp.zeros((BLK, BLK), F32)
    acc1 = jnp.zeros((BLK, BLK), F32)
    for d in range(NDP):
        low = got[d, 4 * LOWIN : 4 * PACK_A, :]
        acc0 = acc0 + dot(tok[:, 2 * d * BLK : (2 * d + 1) * BLK], low)
        acc1 = acc1 + dot(tok[:, (2 * d + 1) * BLK : (2 * d + 2) * BLK], low)
    latent = (acc0[:, :RANK] + acc1[:, RANK:]).astype(BF16)
    lat[...] = latent
    for i in range(4):
        low_share[i] = got[4 * meta[WHO] + i, 4 * LOWIN : 4 * PACK_A, :]

    for s in range(SLOTS):
        acc = jnp.concatenate([dot(latent, mid[s, :RANK]), dot(latent, mid[s, RANK:])], axis=1)
        for k in range(DEPTH):
            p = DEPTH * s + k
            acc = acc + dot(tok[:, span(meta[U_KEY + p])], w_gu[meta[U_POS + p]])
        gate, up = acc[:, :BLK], acc[:, BLK:]
        sig = jax.nn.sigmoid(gate)
        active = gate * sig
        hid[s] = (active * up).astype(BF16)
        act[s, :, :BLK] = up * sig * (1.0 + gate * (1.0 - sig))
        act[s, :, BLK:] = active
    for lane in range(NMP * CAP):
        send[lane // CAP, lane % CAP] = hid[meta[SEND_A + lane]]
    keep.wait()


def up_grads_body(
    meta, got, act, mid, lat, tok_t, perm, grad, gu, part, back_latent, midg, full, sem
):
    latent = lat[...]
    total = got[0, BACK_SUM:].astype(F32)
    for i in range(1, NMP):
        total = total + got[i, BACK_SUM:].astype(F32)
    back = total[:, :RANK].astype(BF16)
    back_latent[...] = back
    latent_t = turned(jnp.concatenate([latent, latent], axis=1))[:RANK]
    lat_sum = jnp.zeros((BLK, RANK), F32)
    for s in range(SLOTS):
        lane = meta[GOT_B + s]
        peer, c = lane // CAP, lane % CAP
        block = got[peer, span(c), :].astype(F32)
        at = pl.multiple_of(BACK_LOW + c * RANK, RANK)
        flow = (block + dot(back, got[peer, pl.ds(at, RANK), :])).astype(BF16).astype(F32)
        gg = (flow * act[s, :, :BLK]).astype(BF16)
        ug = (flow * act[s, :, BLK:]).astype(BF16)
        both = jnp.concatenate([gg, ug], axis=1)
        gu[s] = both
        lat_sum = lat_sum + dot_t(gg, mid[s, :RANK]) + dot_t(ug, mid[s, RANK:])
        two = dot(latent_t, both).astype(BF16)
        midg[s] = jnp.concatenate([two[:, :BLK], two[:, BLK:]], axis=0)
    part[...] = lat_sum

    def store(block, rows):
        full[:, 4 * block : 4 * block + 16, :] = rows.reshape(NDP, 16, BLK)

    zero = jnp.zeros((BLK, BLK), BF16)
    for g in range(11):
        pieces = []
        for j in range(4 * g, 4 * g + 4):
            if j < LIVE:
                piece = dot(tok_t[meta[U_ROW + j]], gu[meta[U_SLOT + j]]).astype(BF16)
            else:
                piece = jnp.concatenate([midg[j - LIVE], zero], axis=1)
            pieces.append(piece)
        both = dot(perm[...], jnp.concatenate(pieces, axis=0)).astype(BF16)
        store(GATE + 4 * g, both[:, :BLK])
        store(UP + 4 * g, both[:, BLK:])
    for i in (2, 6, 10):
        rows = jnp.concatenate([midg[i + jj] for jj in range(4)], axis=0)
        store(MID + i, dot(perm[...], rows).astype(BF16))
    copy = pltpu.make_async_copy(full, grad.at[:, : 4 * GRAD_A, :], sem)
    copy.start()
    copy.wait()


def down_grads_body(
    meta, got, dlin, back_latent, cot, perm, perm2, start, grad, hd, part, hd_t, ding, full, sem
):
    back = back_latent[...]
    back_t = turned(jnp.concatenate([back, back], axis=1))[:RANK]
    down_sum = jnp.zeros((BLK, RANK), F32)
    for t in range(SLOTS):
        lane = meta[GOT_A + t]
        h = got[lane // CAP, lane % CAP]
        hd[t] = h
        hd_t[t] = turned(h)
        down_sum = down_sum + dot_t(h, dlin[t])
        ding[t] = dot(back_t, h).astype(BF16)
    part[...] = down_sum

    def store(block, rows):
        full[:, 4 * block : 4 * block + 16, :] = rows.reshape(NDP, 16, BLK)

    zero = jnp.zeros((BLK, BLK), BF16)

    def tile_of(g):
        pieces = []
        for j in range(4 * g, 4 * g + 4):
            if j < LIVE:
                cols = cot[:, span(meta[D_COL + j])]
                pieces.append(dot(hd_t[meta[D_SLOT + j]], cols).astype(BF16))
            else:
                pieces.append(zero)
        return jnp.concatenate(pieces, axis=0)

    for g in range(0, 11, 2):
        tiles = [i for i in (g, g + 1) if i < 11]
        both = dot(perm[...], jnp.concatenate([tile_of(i) for i in tiles], axis=1)).astype(BF16)
        for half, i in enumerate(tiles):
            store(DOWN + 4 * i, both[:, half * BLK : (half + 1) * BLK])
    none = jnp.zeros((RANK, BLK), BF16)
    left = jnp.concatenate([ding[t] for t in range(8)], axis=0)
    right = jnp.concatenate([ding[t] for t in range(8, SLOTS)] + [none, none], axis=0)
    both = dot(perm2[...], jnp.concatenate([left, right], axis=1)).astype(BF16)
    store(DLIN, both[:, :BLK])
    store(DLIN + 4, both[:, BLK:])
    copy = pltpu.make_async_copy(full, grad.at[:, 4 * GRAD_A :, :], sem)
    copy.start()
    copy.wait()


def token_part_body(meta, gu, w_gu, keep, pass_on, acc):
    acc[...] = jnp.zeros_like(acc)
    for j in range(LIVE):
        r = meta[U_ROW + j]
        acc[r] = acc[r] + dot_t(gu[meta[U_SLOT + j]], w_gu[j])
    y, z = meta[WHO] // 2, lax.rem(meta[WHO], 2)
    for k in range(NY):
        owner = 2 * lax.rem(y + k, NY)
        for e in range(SHARE):
            keep[k, e] = acc[(owner + z) * SHARE + e].astype(BF16)
            pass_on[k, e] = acc[(owner + 1 - z) * SHARE + e].astype(BF16)


def out_part_body(meta, hd, w_d, *rest):
    outs, acc = rest[:NY], rest[NY]
    acc[...] = jnp.zeros_like(acc)
    for j in range(LIVE):
        c = meta[D_COL + j]
        acc[c] = acc[c] + dot(hd[meta[D_SLOT + j]], w_d[j])
    for k in range(NY):
        owner = 2 * lax.rem(meta[WHO] // 2 + k, NY)
        for i in range(2):
            for e in range(SHARE):
                outs[k][i, e] = acc[(owner + i) * SHARE + e].astype(BF16)


def token_pair_body(keep, came, *outs):
    for k in range(NY):
        outs[k][...] = (keep[k].astype(F32) + came[k].astype(F32)).astype(BF16)


def out_y_body(meta, *refs):
    got, (keep, pass_on) = refs[:NY], refs[NY:]
    z = lax.rem(meta[WHO], 2)
    for out, i in ((pass_on, 1 - z), (keep, z)):
        for e in range(SHARE):
            total = got[0][i, e].astype(F32)
            for ref in got[1:]:
                total = total + ref[i, e].astype(F32)
            out[e] = total.astype(BF16)


def small_grads_body(meta, parts, tok_t, cot, perm2, latents, grad):
    total = parts[0].astype(F32)
    for i in range(1, NMP):
        total = total + parts[i].astype(F32)
    total = total.astype(BF16)
    latents[0] = total[:, :RANK]
    latents[1] = total[:, RANK:]
    who = meta[WHO]
    rows = pl.ds(pl.multiple_of((who % 4) * 32, 32), 32)
    order = [(q % 4) * 8 + q // 4 for q in range(NDP)]
    pieces = [tok_t[2 * d + who // 4, rows, :] for d in order]
    low = dot(jnp.concatenate(pieces, axis=0), total[:, :RANK]).reshape(NDP, 32, RANK)
    low = jnp.concatenate([low[:, :16], low[:, 16:]], axis=2)
    grad[:, :16, :] = low.astype(BF16)
    down_t = turned(total)[RANK:]
    pieces = [dot(down_t, cot[:, span(who * SHARE + e)]).astype(BF16) for e in range(SHARE)]
    rows = dot(perm2[...], jnp.concatenate(pieces, axis=0)).astype(BF16)
    grad[:, 16:, :] = rows.reshape(NDP, 16, BLK)


def share_sum(refs, e):
    total = refs[0][e].astype(F32)
    for ref in refs[1:]:
        total = total + ref[e].astype(F32)
    return total


def token_out_body(*refs):
    got, (latents, low_share, out) = refs[:NY], refs[NY:]
    latent = latents[0]
    for e in range(SHARE):
        low = low_share[e // 2]
        low = low[:, :RANK] if e % 2 == 0 else low[:, RANK:]
        out[:, e * BLK : (e + 1) * BLK] = (share_sum(got, e) + dot_t(latent, low)).astype(BF16)


def layer_out_body(keep, came, latents, dlout, out):
    latent = latents[1]
    for e in range(SHARE):
        low = dot(latent, dlout[e * RANK : (e + 1) * RANK])
        out[:, e * BLK : (e + 1) * BLK] = (share_sum((keep, came), e) + low).astype(BF16)


def final_body(up_count, down_count, who, got, gate_o, up_o, down_o, mid_o, tail, red):
    total = got[0, :GRAD].astype(F32)
    for i in range(1, 4):
        total = total + got[i, :GRAD].astype(F32)
    red[...] = total.astype(BF16)
    mine = who[0] * SLOTS
    zero = jnp.zeros((4, BLK), BF16)

    def put(out, counts, base):
        at = jnp.int32(base)
        for s in range(SLOTS):
            count = counts[mine + s]
            for k in range(DEPTH):
                out[s, k] = jnp.where(k < count, red[at], zero)
                at = at + (k < count).astype(I32)

    put(gate_o, up_count, GATE)
    put(up_o, up_count, UP)
    put(down_o, down_count, GRAD_A + DOWN)
    for s in range(SLOTS):
        mid_o[:, s * BLK : (s + 1) * BLK] = red[MID + s]
    for e in range(8):
        tail[e] = red[GRAD_A + DLIN + e]


def lookup(table_ids, positions):
    span_ids = jnp.arange(table_ids.shape[0], dtype=I32)
    return jnp.sum(jnp.where(positions[..., None] == span_ids, table_ids, 0), axis=-1)


def own_rows(table_ids, mine):
    return lax.dynamic_slice_in_dim(table_ids, mine * SLOTS, SLOTS, 0)


def inverse_of(order_ids):
    ids = jnp.arange(order_ids.shape[0], dtype=I32)
    return jnp.sum(jnp.where(order_ids[None, :] == ids[:, None], ids[None, :], 0), axis=1)


def send_table(owner, peer, rank, local_slot, mine):
    lanes = jnp.arange(NMP * CAP, dtype=I32)
    target = peer * CAP + rank
    matched = (owner[None, :] == mine) & (target[None, :] == lanes[:, None])
    return jnp.sum(jnp.where(matched, local_slot[None, :], 0), axis=1)


def live_table(count, keys):
    live = (jnp.arange(DEPTH, dtype=I32)[None, :] < count[:, None]).reshape(-1)
    ids = jnp.arange(SLOTS * DEPTH, dtype=I32)
    place = jnp.sum(jnp.where((ids[None, :] < ids[:, None]) & live[None, :], 1, 0), axis=1)
    hit = (jnp.arange(LIVE, dtype=I32)[:, None] == place[None, :]) & live[None, :]
    flat = keys.reshape(-1)
    of_key = jnp.sum(jnp.where(hit, flat[None, :], 0), axis=1)
    of_slot = jnp.sum(jnp.where(hit, (ids // DEPTH)[None, :], 0), axis=1)
    return of_key, of_slot, flat, jnp.where(live, place, LIVE)


def tables(mine, up_order, down_order, up_rows, down_cols, up_count, down_count):
    slot_ids = jnp.arange(up_order.shape[0], dtype=I32)
    source = lookup(inverse_of(up_order), down_order)
    from_device, to_device = source // SLOTS, slot_ids // SLOTS
    earlier = (
        (from_device[None, :] == from_device[:, None])
        & (to_device[None, :] == to_device[:, None])
        & (slot_ids[None, :] < slot_ids[:, None])
    )
    rank = jnp.sum(earlier.astype(I32), axis=1)
    send_a = send_table(from_device, to_device, rank, source % SLOTS, mine)
    got_a = own_rows(from_device * CAP + rank, mine)
    send_b = send_table(to_device, from_device, rank, slot_ids % SLOTS, mine)
    blocks_down = lookup(inverse_of(down_order), own_rows(up_order, mine))
    got_b = lookup(to_device * CAP + rank, blocks_down)
    u = live_table(own_rows(up_count, mine), own_rows(up_rows, mine))
    d = live_table(own_rows(down_count, mine), own_rows(down_cols, mine))
    fields = [
        (U_ROW, u[0]), (U_SLOT, u[1]), (D_COL, d[0]), (D_SLOT, d[1]), (U_KEY, u[2]), (D_KEY, d[2]),
        (U_POS, u[3]), (D_POS, d[3]), (SEND_A, send_a), (SEND_B, send_b), (GOT_A, got_a),
        (GOT_B, got_b), (WHO, mine.reshape(1)),
    ]
    ends = [start for start, _ in fields[1:]] + [META]
    padded = [jnp.pad(v, (0, end - start - v.shape[0])) for (start, v), end in zip(fields, ends)]
    return jnp.concatenate(padded)


def permutations():
    r = jnp.arange(512, dtype=I32)
    q, rest = r // 16, r % 16
    plain = q
    chain = (q % 4) * 8 + (q // 4 % 4) * 2 + q // 16
    give = (q % 4) * 8 + q // 4
    row4 = lambda d: (rest // 4) * BLK + 4 * d + rest % 4
    row2 = lambda d: (rest // 2) * RANK + 2 * d + rest % 2
    out = lambda src: (src[:, None] == r[None, :]).astype(BF16)
    into = lambda src: (src[None, :] == r[:, None]).astype(BF16)
    return (
        into(row4(plain)), into(row4(chain)), into(row2(chain)),
        out(row4(give)), out(row2(give)),
    )


def spread(x, axis, n):
    return lax.all_to_all(jnp.broadcast_to(x[None], (n,) + x.shape), axis, 0, 0, tiled=True)


def gather_step(x, axis, n):
    x = spread(x, axis, n)
    return x.reshape((-1,) + x.shape[-2:])


def together(values):
    return lax.optimization_barrier(values)


def rotate(parts):
    moved = [
        lax.ppermute(parts[k], "y", [(i, (i + k) % NY) for i in range(NY)]) for k in range(1, NY)
    ]
    return [parts[0]] + moved


def local(
    tokens, cotangent, gate_weight, up_weight, down_weight, low_in, low_mid, down_low_in,
    down_low_out, up_order, down_order, up_rows, down_cols, up_count, down_count,
):
    mine = lax.axis_index(MP).astype(I32)
    who = mine.reshape(1)
    low_rows = jnp.concatenate([low_in[:BLK], low_in[BLK:]], axis=1).reshape(32, 4, BLK)
    first = call(
        pack_up_body, shape(PACK_A, 4, BLK), (gate_weight, up_weight, low_mid, low_rows),
        (up_count, who),
    )
    first, down_low_in, down_low_out = together((first, down_low_in, down_low_out))
    dlin_rows = jnp.pad(
        down_low_in.reshape(2, SLOTS, BLK).transpose(1, 0, 2).reshape(2 * SLOTS, BLK), ((0, 4), (0, 0))
    ).reshape(8, 4, BLK)
    dlout_rows = down_low_out.reshape(2, SHARE, BLK).transpose(1, 0, 2).reshape(4, 4, BLK)
    second = call(
        pack_down_body, shape(PACK_B, 4, BLK), (down_weight, dlin_rows, dlout_rows),
        (down_count, who),
    )
    got_up = lax.all_gather(first.reshape(4 * PACK_A, BLK), DP)
    got_down = gather_step(second.reshape(1, 4 * PACK_B, BLK), "zh", 4)
    ids = (mine, up_order, down_order, up_rows, down_cols, up_count, down_count)
    got_down, ids = together((got_down, ids))
    got_down = gather_step(got_down, "x", 4)
    meta = tables(*ids)
    take, take_c, take2_c, give, give2 = permutations()
    got_down, meta = together((got_down, meta))
    got_down = gather_step(got_down, "core", 2)
    tok_t = tokens.reshape(BLK, COLS, BLK).transpose(1, 2, 0)

    slots = shape(SLOTS, BLK, BLK)
    slots_scratch = pltpu.VMEM((SLOTS, BLK, BLK), BF16)
    parcel = shape(NMP, CAP, BLK, BLK)
    got_down, take, give, give2 = together((got_down, take, give, give2))
    back_send, w_d, dlin, dlout = call(
        hidden_grad_body,
        (
            shape(NMP, BACK_ROWS, BLK), shape(LIVE + 1, BLK, BLK), shape(SLOTS, RANK, BLK),
            shape(512, BLK),
        ),
        (got_down, cotangent, take_c, take2_c), (meta,), (slots_scratch,),
    )
    back_send, tok_t = together((back_send, tok_t))
    back_got = lax.all_to_all(back_send, MP, 0, 0, tiled=True)

    hbm = pl.BlockSpec(memory_space=pl.ANY)
    vmem = pl.BlockSpec(memory_space=pltpu.VMEM)
    smem = pl.BlockSpec(memory_space=pltpu.SMEM)
    weights = (LIVE + 1, BLK, 2 * BLK)
    send, act, w_gu, mid, lat, low_share = pl.pallas_call(
        forward_body,
        out_shape=(
            parcel, shape(SLOTS, BLK, 2 * BLK, dtype=F32), shape(*weights), slots,
            shape(BLK, RANK), shape(4, BLK, BLK),
        ),
        in_specs=[smem, hbm, hbm, vmem],
        out_specs=(vmem, vmem, hbm, vmem, vmem, vmem),
        scratch_shapes=[
            slots_scratch, pltpu.VMEM((NDP, 4 * PACK_A, BLK), BF16),
            pltpu.VMEM((BLK, COLS * BLK), BF16), pltpu.VMEM(weights, BF16),
            pltpu.SemaphoreType.DMA((4,)),
        ],
        compiler_params=pltpu.CompilerParams(vmem_limit_bytes=VMEM_LIMIT),
    )(meta, got_up, tokens, take)
    got = lax.all_to_all(send, MP, 0, 0, tiled=True)

    grad_shape = shape(NDP, 4 * GRAD, BLK)
    grad, gu, part_up, back_latent = pl.pallas_call(
        up_grads_body,
        out_shape=(
            grad_shape, shape(SLOTS, BLK, 2 * BLK), shape(BLK, RANK, dtype=F32), shape(BLK, RANK),
        ),
        in_specs=[smem] + [vmem] * 6,
        out_specs=(hbm, vmem, vmem, vmem),
        scratch_shapes=[
            slots_scratch, pltpu.VMEM((NDP, 4 * GRAD_A, BLK), BF16), pltpu.SemaphoreType.DMA,
        ],
        compiler_params=pltpu.CompilerParams(vmem_limit_bytes=VMEM_LIMIT),
    )(meta, back_got, act, mid, lat, tok_t, give)
    grad, hd, part_down = pl.pallas_call(
        down_grads_body,
        out_shape=(grad_shape, slots, shape(BLK, RANK, dtype=F32)),
        in_specs=[smem] + [vmem] * 6 + [hbm],
        out_specs=(hbm, vmem, vmem),
        scratch_shapes=[
            slots_scratch, pltpu.VMEM((SLOTS, RANK, BLK), BF16),
            pltpu.VMEM((NDP, 4 * (GRAD - GRAD_A), BLK), BF16), pltpu.SemaphoreType.DMA,
        ],
        input_output_aliases={7: 0},
        compiler_params=pltpu.CompilerParams(vmem_limit_bytes=VMEM_LIMIT),
    )(meta, got, dlin, back_latent, cotangent, give, give2, grad)
    grad = lax.psum_scatter(
        grad.reshape(NDP * 4 * GRAD, BLK), ("x", "core"), scatter_dimension=0, tiled=True
    )
    part = jnp.concatenate([part_up, part_down], axis=1).astype(BF16)
    parts = spread(part, MP, NMP)
    acc = pltpu.VMEM((COLS, BLK, BLK), F32)
    token_part = call(
        token_part_body, (shape(NY, SHARE, BLK, BLK),) * 2, (gu, w_gu), (meta,), (acc,)
    )
    out_part = call(
        out_part_body, (shape(2, SHARE, BLK, BLK),) * NY, (hd, w_d), (meta,), (acc,)
    )
    parts, token_part, out_part = together((parts, token_part, out_part))
    latents, small = call(
        small_grads_body, (shape(2, BLK, RANK), shape(NDP, 32, BLK)),
        (parts, tok_t, cotangent, give2), (meta,),
    )

    swap = [(0, 1), (1, 0)]
    token_came = lax.ppermute(token_part[1], "zl", swap)
    out_got = rotate(out_part)
    small = lax.all_to_all(small.reshape(8, BLK, BLK), ("x", "core"), 0, 0, tiled=True)
    small = jnp.sum(small.astype(F32), axis=0).astype(BF16).reshape(4, 32, BLK)
    small, grad, token_came, out_got = together((small, grad, token_came, out_got))
    grad = jnp.concatenate([grad.reshape(4, 4 * GRAD, BLK), small], axis=1)
    grad = lax.all_to_all(grad, "zh", 0, 0, tiled=True)
    half = shape(SHARE, BLK, BLK)
    out_keep, out_give = call(out_y_body, (half,) * 2, out_got, (meta,))
    token_came, out_give = together((token_came, out_give))
    out_came = lax.ppermute(out_give, "zl", swap)
    token_got = rotate(call(token_pair_body, (half,) * NY, (token_part[0], token_came), ()))
    wide = shape(BLK, SHARE * BLK)
    token_grad = call(token_out_body, wide, (*token_got, latents, low_share), ())
    layer_out = call(layer_out_body, wide, (out_keep, out_came, latents, dlout), ())
    grad, token_grad, layer_out = together((grad, token_grad, layer_out))
    small = jnp.sum(grad[:, 4 * GRAD :].astype(F32), axis=0).astype(BF16)
    low_g = spread(small[:16], MP, NMP)
    wide = shape(SLOTS, DEPTH, 4, BLK)
    gate_g, up_g, down_g, mid_g, tail = call(
        final_body, (wide, wide, wide, shape(4, SLOTS * BLK), shape(8, 4, BLK)),
        (grad.reshape(4, GRAD + 8, 4, BLK),), (up_count, down_count, who),
        (pltpu.VMEM((GRAD, 4, BLK), BF16),),
    )
    dlin_g = tail.reshape(16, 2, BLK)[:SLOTS].transpose(1, 0, 2).reshape(2, SLOTS * BLK)
    low_g = jnp.concatenate([low_g[:, :, :RANK], low_g[:, :, RANK:]], axis=1)
    low_in_grad = low_g.reshape(2 * BLK, RANK)
    dlout_g = small[16:].reshape(SHARE, 2, BLK).transpose(1, 0, 2).reshape(2, SHARE * BLK)
    return layer_out, token_grad, gate_g, up_g, down_g, low_in_grad, mid_g, dlin_g, dlout_g


def solution(mesh):
    fine = Mesh(mesh.devices.reshape(4, 4, 2, 4, 2), DP + MP)
    rows, both, blocks = P(DP, None), P(DP, MP), P(MP, None, DP, None)
    in_specs = (rows, rows, blocks, blocks, blocks, rows, both, both, both) + (P(),) * 6
    out_specs = (both, both, blocks, blocks, blocks, rows, both, both, both)
    return jax.shard_map(local, mesh=fine, in_specs=in_specs, out_specs=out_specs, check_vma=False)
```

```python
import jax
import jax.numpy as jnp
from jax import lax
from jax.experimental import pallas as pl
from jax.experimental.pallas import tpu as pltpu
from jax.sharding import Mesh, PartitionSpec as P

F32 = jnp.float32
BF16 = jnp.bfloat16
I32 = jnp.int32
DP = ("zh", "x", "core")
MP = ("y", "zl")
NDP, NMP = 32, 8
SLOTS, DEPTH, BLK = 14, 5, 128
LIVE = 42
RANK = 64
COLS = 64
SHARE = COLS // NMP
CAP = 2
NY = 4
BACK_LOW = CAP * BLK
BACK_SUM = BACK_LOW + CAP * RANK
BACK_ROWS = BACK_SUM + BLK
VMEM_LIMIT = 58 * 2**20

GATE, MID, UP, LOWIN, PACK_A = 0, 42, 56, 100, 132
DOWN, DLIN, DLOUT, PACK_B = 0, 44, 52, 56
GRAD_A, GRAD = 100, 152

U_ROW, U_SLOT, D_COL, D_SLOT = 0, 48, 96, 144
U_KEY, D_KEY, U_POS, D_POS = 192, 264, 336, 408
SEND_A, SEND_B, GOT_A, GOT_B, WHO, META = 480, 496, 512, 528, 544, 560


def dot(a, b):
    return lax.dot_general(a, b, (((1,), (0,)), ((), ())), preferred_element_type=F32)


def dot_t(a, b):
    return lax.dot_general(a, b, (((1,), (1,)), ((), ())), preferred_element_type=F32)


def turned(a):
    return a.astype(F32).T.astype(BF16)


def span(start):
    return pl.ds(pl.multiple_of(start * BLK, BLK), BLK)


def call(body, out_shapes, operands, scalars, scratch=()):
    vmem = pl.BlockSpec(memory_space=pltpu.VMEM)
    smem = pl.BlockSpec(memory_space=pltpu.SMEM)
    return pl.pallas_call(
        body,
        out_shape=out_shapes,
        in_specs=[smem] * len(scalars) + [vmem] * len(operands),
        out_specs=jax.tree.map(lambda _: vmem, out_shapes),
        scratch_shapes=list(scratch),
        compiler_params=pltpu.CompilerParams(vmem_limit_bytes=VMEM_LIMIT),
    )(*scalars, *operands)


def shape(*dims, dtype=BF16):
    return jax.ShapeDtypeStruct(dims, dtype)


def put_live(out, weight, counts, mine, base):
    at = jnp.int32(base)
    for s in range(SLOTS):
        count = counts[mine + s]
        for k in range(DEPTH):
            out[at] = weight[s, k]
            at = at + (k < count).astype(I32)


def pack_up_body(up_count, who, gate_w, up_w, mid, low, out):
    mine = who[0] * SLOTS
    for pad in (UP + 42, UP + 43):
        out[pad] = jnp.zeros((4, BLK), BF16)
    put_live(out, gate_w, up_count, mine, GATE)
    put_live(out, up_w, up_count, mine, UP)
    for s in range(SLOTS):
        out[MID + s] = mid[:, s * BLK : (s + 1) * BLK]
    for e in range(32):
        out[LOWIN + e] = low[e]


def pack_down_body(down_count, who, down_w, dlin, dlout, out):
    for pad in (DOWN + 42, DOWN + 43):
        out[pad] = jnp.zeros((4, BLK), BF16)
    put_live(out, down_w, down_count, who[0] * SLOTS, DOWN)
    for e in range(8):
        out[DLIN + e] = dlin[e]
    for e in range(4):
        out[DLOUT + e] = dlout[e]


def hidden_grad_body(meta, got, cot, perm, perm2, send, w_d, dlin, dlout, hgrad):
    def rows(block):
        return got[:, 4 * block : 4 * block + 16, :].reshape(512, BLK)

    for g in range(0, 11, 2):
        blocks = [DOWN + 4 * i for i in (g, g + 1) if i < 11]
        both = dot(perm[...], jnp.concatenate([rows(b) for b in blocks], axis=1)).astype(BF16)
        for half in range(len(blocks)):
            for jj in range(4):
                j = 4 * (g + half) + jj
                if j < LIVE:
                    w_d[j] = both[jj * BLK : (jj + 1) * BLK, half * BLK : (half + 1) * BLK]
    w_d[LIVE] = jnp.zeros((BLK, BLK), BF16)
    joined = jnp.concatenate([rows(DLIN), rows(DLIN + 4)], axis=1)
    both = dot(perm2[...], joined).astype(BF16)
    for t in range(SLOTS):
        dlin[t] = both[(t % 8) * RANK : (t % 8 + 1) * RANK, (t // 8) * BLK : (t // 8 + 1) * BLK]
    who = meta[WHO] * SHARE
    low = dot(perm2[...], rows(DLOUT)).astype(BF16)
    dlout[...] = low
    total = jnp.zeros((BLK, RANK), F32)
    for e in range(SHARE):
        total = total + dot_t(cot[:, span(who + e)], low[e * RANK : (e + 1) * RANK])
    total = jnp.concatenate([total, jnp.zeros_like(total)], axis=1).astype(BF16)
    for t in range(SLOTS):
        acc = jnp.zeros((BLK, BLK), F32)
        for k in range(DEPTH):
            p = DEPTH * t + k
            acc = acc + dot_t(cot[:, span(meta[D_KEY + p])], w_d[meta[D_POS + p]])
        hgrad[t] = acc.astype(BF16)
    for lane in range(NMP * CAP):
        peer, c = lane // CAP, lane % CAP
        t = meta[SEND_B + lane]
        send[peer, c * BLK : (c + 1) * BLK] = hgrad[t]
        send[peer, BACK_LOW + c * RANK : BACK_LOW + (c + 1) * RANK] = dlin[t]
    for peer in range(NMP):
        send[peer, BACK_SUM:] = total


def forward_body(
    meta, got_far, tok_far, perm, send, act, w_far, mid, lat, low_share, hid, got, tok, w_gu, sems
):
    loads = [
        pltpu.make_async_copy(
            got_far.at[:, : 4 * LOWIN, :], got.at[:, : 4 * LOWIN, :], sems.at[0]
        ),
        pltpu.make_async_copy(
            got_far.at[:, 4 * LOWIN :, :], got.at[:, 4 * LOWIN :, :], sems.at[1]
        ),
        pltpu.make_async_copy(tok_far, tok, sems.at[2]),
    ]
    for load in loads:
        load.start()
    loads[0].wait()

    def rows(block):
        return got[:, 4 * block : 4 * block + 16, :].reshape(512, BLK)

    def pair(first, second):
        joined = jnp.concatenate([rows(first), rows(second)], axis=1)
        return dot(perm[...], joined).astype(BF16)

    for g in range(11):
        both = pair(GATE + 4 * g, UP + 4 * g)
        for jj in range(4):
            piece = both[jj * BLK : (jj + 1) * BLK]
            if 4 * g + jj < LIVE:
                w_gu[4 * g + jj] = piece
            else:
                mid[4 * g + jj - LIVE] = piece[:, :BLK]
    w_gu[LIVE] = jnp.zeros((BLK, 2 * BLK), BF16)
    for a, b in ((2, 6), (10, 10)):
        both = pair(MID + a, MID + b)
        for half, i in enumerate((a, b)[: 1 + (a != b)]):
            for jj in range(4):
                mid[i + jj] = both[jj * BLK : (jj + 1) * BLK, half * BLK : (half + 1) * BLK]
    keep = pltpu.make_async_copy(w_gu, w_far, sems.at[3])
    keep.start()
    loads[1].wait()
    loads[2].wait()

    acc0 = jnp.zeros((BLK, BLK), F32)
    acc1 = jnp.zeros((BLK, BLK), F32)
    for d in range(NDP):
        low = got[d, 4 * LOWIN : 4 * PACK_A, :]
        acc0 = acc0 + dot(tok[:, 2 * d * BLK : (2 * d + 1) * BLK], low)
        acc1 = acc1 + dot(tok[:, (2 * d + 1) * BLK : (2 * d + 2) * BLK], low)
    latent = (acc0[:, :RANK] + acc1[:, RANK:]).astype(BF16)
    lat[...] = latent
    for i in range(4):
        low_share[i] = got[4 * meta[WHO] + i, 4 * LOWIN : 4 * PACK_A, :]

    for s in range(SLOTS):
        acc = jnp.concatenate([dot(latent, mid[s, :RANK]), dot(latent, mid[s, RANK:])], axis=1)
        for k in range(DEPTH):
            p = DEPTH * s + k
            acc = acc + dot(tok[:, span(meta[U_KEY + p])], w_gu[meta[U_POS + p]])
        gate, up = acc[:, :BLK], acc[:, BLK:]
        sig = jax.nn.sigmoid(gate)
        active = gate * sig
        hid[s] = (active * up).astype(BF16)
        act[s, :, :BLK] = up * sig * (1.0 + gate * (1.0 - sig))
        act[s, :, BLK:] = active
    for lane in range(NMP * CAP):
        send[lane // CAP, lane % CAP] = hid[meta[SEND_A + lane]]
    keep.wait()


def up_grads_body(
    meta, got, act, mid, lat, tok_t, perm, grad, gu, part, back_latent, midg, full, sem
):
    latent = lat[...]
    total = got[0, BACK_SUM:].astype(F32)
    for i in range(1, NMP):
        total = total + got[i, BACK_SUM:].astype(F32)
    back = total[:, :RANK].astype(BF16)
    back_latent[...] = back
    latent_t = turned(jnp.concatenate([latent, latent], axis=1))[:RANK]
    lat_sum = jnp.zeros((BLK, RANK), F32)
    for s in range(SLOTS):
        lane = meta[GOT_B + s]
        peer, c = lane // CAP, lane % CAP
        block = got[peer, span(c), :].astype(F32)
        at = pl.multiple_of(BACK_LOW + c * RANK, RANK)
        flow = (block + dot(back, got[peer, pl.ds(at, RANK), :])).astype(BF16).astype(F32)
        gg = (flow * act[s, :, :BLK]).astype(BF16)
        ug = (flow * act[s, :, BLK:]).astype(BF16)
        both = jnp.concatenate([gg, ug], axis=1)
        gu[s] = both
        lat_sum = lat_sum + dot_t(gg, mid[s, :RANK]) + dot_t(ug, mid[s, RANK:])
        two = dot(latent_t, both).astype(BF16)
        midg[s] = jnp.concatenate([two[:, :BLK], two[:, BLK:]], axis=0)
    part[...] = lat_sum

    def store(block, rows):
        full[:, 4 * block : 4 * block + 16, :] = rows.reshape(NDP, 16, BLK)

    zero = jnp.zeros((BLK, BLK), BF16)
    for g in range(11):
        pieces = []
        for j in range(4 * g, 4 * g + 4):
            if j < LIVE:
                piece = dot(tok_t[meta[U_ROW + j]], gu[meta[U_SLOT + j]]).astype(BF16)
            else:
                piece = jnp.concatenate([midg[j - LIVE], zero], axis=1)
            pieces.append(piece)
        both = dot(perm[...], jnp.concatenate(pieces, axis=0)).astype(BF16)
        store(GATE + 4 * g, both[:, :BLK])
        store(UP + 4 * g, both[:, BLK:])
    for i in (2, 6, 10):
        rows = jnp.concatenate([midg[i + jj] for jj in range(4)], axis=0)
        store(MID + i, dot(perm[...], rows).astype(BF16))
    copy = pltpu.make_async_copy(full, grad.at[:, : 4 * GRAD_A, :], sem)
    copy.start()
    copy.wait()


def down_grads_body(
    meta, got, dlin, back_latent, cot, perm, perm2, start, grad, hd, part, hd_t, ding, full, sem
):
    back = back_latent[...]
    back_t = turned(jnp.concatenate([back, back], axis=1))[:RANK]
    down_sum = jnp.zeros((BLK, RANK), F32)
    for t in range(SLOTS):
        lane = meta[GOT_A + t]
        h = got[lane // CAP, lane % CAP]
        hd[t] = h
        hd_t[t] = turned(h)
        down_sum = down_sum + dot_t(h, dlin[t])
        ding[t] = dot(back_t, h).astype(BF16)
    part[...] = down_sum

    def store(block, rows):
        full[:, 4 * block : 4 * block + 16, :] = rows.reshape(NDP, 16, BLK)

    zero = jnp.zeros((BLK, BLK), BF16)

    def tile_of(g):
        pieces = []
        for j in range(4 * g, 4 * g + 4):
            if j < LIVE:
                cols = cot[:, span(meta[D_COL + j])]
                pieces.append(dot(hd_t[meta[D_SLOT + j]], cols).astype(BF16))
            else:
                pieces.append(zero)
        return jnp.concatenate(pieces, axis=0)

    for g in range(0, 11, 2):
        tiles = [i for i in (g, g + 1) if i < 11]
        both = dot(perm[...], jnp.concatenate([tile_of(i) for i in tiles], axis=1)).astype(BF16)
        for half, i in enumerate(tiles):
            store(DOWN + 4 * i, both[:, half * BLK : (half + 1) * BLK])
    none = jnp.zeros((RANK, BLK), BF16)
    left = jnp.concatenate([ding[t] for t in range(8)], axis=0)
    right = jnp.concatenate([ding[t] for t in range(8, SLOTS)] + [none, none], axis=0)
    both = dot(perm2[...], jnp.concatenate([left, right], axis=1)).astype(BF16)
    store(DLIN, both[:, :BLK])
    store(DLIN + 4, both[:, BLK:])
    copy = pltpu.make_async_copy(full, grad.at[:, 4 * GRAD_A :, :], sem)
    copy.start()
    copy.wait()


def token_part_body(meta, gu, w_gu, keep, pass_on, acc):
    acc[...] = jnp.zeros_like(acc)
    for j in range(LIVE):
        r = meta[U_ROW + j]
        acc[r] = acc[r] + dot_t(gu[meta[U_SLOT + j]], w_gu[j])
    y, z = meta[WHO] // 2, lax.rem(meta[WHO], 2)
    for k in range(NY):
        owner = 2 * lax.rem(y + k, NY)
        for e in range(SHARE):
            keep[k, e] = acc[(owner + z) * SHARE + e].astype(BF16)
            pass_on[k, e] = acc[(owner + 1 - z) * SHARE + e].astype(BF16)


def out_part_body(meta, hd, w_d, *rest):
    outs, acc = rest[:NY], rest[NY]
    acc[...] = jnp.zeros_like(acc)
    for j in range(LIVE):
        c = meta[D_COL + j]
        acc[c] = acc[c] + dot(hd[meta[D_SLOT + j]], w_d[j])
    for k in range(NY):
        owner = 2 * lax.rem(meta[WHO] // 2 + k, NY)
        for i in range(2):
            for e in range(SHARE):
                outs[k][i, e] = acc[(owner + i) * SHARE + e].astype(BF16)


def token_pair_body(keep, came, *outs):
    for k in range(NY):
        outs[k][...] = (keep[k].astype(F32) + came[k].astype(F32)).astype(BF16)


def out_y_body(meta, *refs):
    got, (keep, pass_on) = refs[:NY], refs[NY:]
    z = lax.rem(meta[WHO], 2)
    for out, i in ((pass_on, 1 - z), (keep, z)):
        for e in range(SHARE):
            total = got[0][i, e].astype(F32)
            for ref in got[1:]:
                total = total + ref[i, e].astype(F32)
            out[e] = total.astype(BF16)


def small_grads_body(meta, parts, tok_t, cot, perm2, latents, grad):
    total = parts[0].astype(F32)
    for i in range(1, NMP):
        total = total + parts[i].astype(F32)
    total = total.astype(BF16)
    latents[0] = total[:, :RANK]
    latents[1] = total[:, RANK:]
    who = meta[WHO]
    rows = pl.ds(pl.multiple_of((who % 4) * 32, 32), 32)
    order = [(q % 4) * 8 + q // 4 for q in range(NDP)]
    pieces = [tok_t[2 * d + who // 4, rows, :] for d in order]
    low = dot(jnp.concatenate(pieces, axis=0), total[:, :RANK]).reshape(NDP, 32, RANK)
    low = jnp.concatenate([low[:, :16], low[:, 16:]], axis=2)
    grad[:, :16, :] = low.astype(BF16)
    down_t = turned(total)[RANK:]
    pieces = [dot(down_t, cot[:, span(who * SHARE + e)]).astype(BF16) for e in range(SHARE)]
    rows = dot(perm2[...], jnp.concatenate(pieces, axis=0)).astype(BF16)
    grad[:, 16:, :] = rows.reshape(NDP, 16, BLK)


def share_sum(refs, e):
    total = refs[0][e].astype(F32)
    for ref in refs[1:]:
        total = total + ref[e].astype(F32)
    return total


def token_out_body(*refs):
    got, (latents, low_share, out) = refs[:NY], refs[NY:]
    latent = latents[0]
    for e in range(SHARE):
        low = low_share[e // 2]
        low = low[:, :RANK] if e % 2 == 0 else low[:, RANK:]
        out[:, e * BLK : (e + 1) * BLK] = (share_sum(got, e) + dot_t(latent, low)).astype(BF16)


def layer_out_body(keep, came, latents, dlout, out):
    latent = latents[1]
    for e in range(SHARE):
        low = dot(latent, dlout[e * RANK : (e + 1) * RANK])
        out[:, e * BLK : (e + 1) * BLK] = (share_sum((keep, came), e) + low).astype(BF16)


def final_body(up_count, down_count, who, got, gate_o, up_o, down_o, mid_o, tail, red):
    total = got[0, :GRAD].astype(F32)
    for i in range(1, 4):
        total = total + got[i, :GRAD].astype(F32)
    red[...] = total.astype(BF16)
    mine = who[0] * SLOTS
    zero = jnp.zeros((4, BLK), BF16)

    def put(out, counts, base):
        at = jnp.int32(base)
        for s in range(SLOTS):
            count = counts[mine + s]
            for k in range(DEPTH):
                out[s, k] = jnp.where(k < count, red[at], zero)
                at = at + (k < count).astype(I32)

    put(gate_o, up_count, GATE)
    put(up_o, up_count, UP)
    put(down_o, down_count, GRAD_A + DOWN)
    for s in range(SLOTS):
        mid_o[:, s * BLK : (s + 1) * BLK] = red[MID + s]
    for e in range(8):
        tail[e] = red[GRAD_A + DLIN + e]


def lookup(table_ids, positions):
    span_ids = jnp.arange(table_ids.shape[0], dtype=I32)
    return jnp.sum(jnp.where(positions[..., None] == span_ids, table_ids, 0), axis=-1)


def own_rows(table_ids, mine):
    return lax.dynamic_slice_in_dim(table_ids, mine * SLOTS, SLOTS, 0)


def inverse_of(order_ids):
    ids = jnp.arange(order_ids.shape[0], dtype=I32)
    return jnp.sum(jnp.where(order_ids[None, :] == ids[:, None], ids[None, :], 0), axis=1)


def send_table(owner, peer, rank, local_slot, mine):
    lanes = jnp.arange(NMP * CAP, dtype=I32)
    target = peer * CAP + rank
    matched = (owner[None, :] == mine) & (target[None, :] == lanes[:, None])
    return jnp.sum(jnp.where(matched, local_slot[None, :], 0), axis=1)


def live_table(count, keys):
    live = (jnp.arange(DEPTH, dtype=I32)[None, :] < count[:, None]).reshape(-1)
    ids = jnp.arange(SLOTS * DEPTH, dtype=I32)
    place = jnp.sum(jnp.where((ids[None, :] < ids[:, None]) & live[None, :], 1, 0), axis=1)
    hit = (jnp.arange(LIVE, dtype=I32)[:, None] == place[None, :]) & live[None, :]
    flat = keys.reshape(-1)
    of_key = jnp.sum(jnp.where(hit, flat[None, :], 0), axis=1)
    of_slot = jnp.sum(jnp.where(hit, (ids // DEPTH)[None, :], 0), axis=1)
    return of_key, of_slot, flat, jnp.where(live, place, LIVE)


def tables(mine, up_order, down_order, up_rows, down_cols, up_count, down_count):
    slot_ids = jnp.arange(up_order.shape[0], dtype=I32)
    source = lookup(inverse_of(up_order), down_order)
    from_device, to_device = source // SLOTS, slot_ids // SLOTS
    earlier = (
        (from_device[None, :] == from_device[:, None])
        & (to_device[None, :] == to_device[:, None])
        & (slot_ids[None, :] < slot_ids[:, None])
    )
    rank = jnp.sum(earlier.astype(I32), axis=1)
    send_a = send_table(from_device, to_device, rank, source % SLOTS, mine)
    got_a = own_rows(from_device * CAP + rank, mine)
    send_b = send_table(to_device, from_device, rank, slot_ids % SLOTS, mine)
    blocks_down = lookup(inverse_of(down_order), own_rows(up_order, mine))
    got_b = lookup(to_device * CAP + rank, blocks_down)
    u = live_table(own_rows(up_count, mine), own_rows(up_rows, mine))
    d = live_table(own_rows(down_count, mine), own_rows(down_cols, mine))
    fields = [
        (U_ROW, u[0]), (U_SLOT, u[1]), (D_COL, d[0]), (D_SLOT, d[1]), (U_KEY, u[2]), (D_KEY, d[2]),
        (U_POS, u[3]), (D_POS, d[3]), (SEND_A, send_a), (SEND_B, send_b), (GOT_A, got_a),
        (GOT_B, got_b), (WHO, mine.reshape(1)),
    ]
    ends = [start for start, _ in fields[1:]] + [META]
    padded = [jnp.pad(v, (0, end - start - v.shape[0])) for (start, v), end in zip(fields, ends)]
    return jnp.concatenate(padded)


def permutations():
    r = jnp.arange(512, dtype=I32)
    q, rest = r // 16, r % 16
    plain = q
    chain = (q % 4) * 8 + (q // 4 % 4) * 2 + q // 16
    give = (q % 4) * 8 + q // 4
    row4 = lambda d: (rest // 4) * BLK + 4 * d + rest % 4
    row2 = lambda d: (rest // 2) * RANK + 2 * d + rest % 2
    out = lambda src: (src[:, None] == r[None, :]).astype(BF16)
    into = lambda src: (src[None, :] == r[:, None]).astype(BF16)
    return (
        into(row4(plain)), into(row4(chain)), into(row2(chain)),
        out(row4(give)), out(row2(give)),
    )


def spread(x, axis, n):
    return lax.all_to_all(jnp.broadcast_to(x[None], (n,) + x.shape), axis, 0, 0, tiled=True)


def gather_step(x, axis, n):
    x = spread(x, axis, n)
    return x.reshape((-1,) + x.shape[-2:])


def together(values):
    return lax.optimization_barrier(values)


def rotate(parts):
    moved = [
        lax.ppermute(parts[k], "y", [(i, (i + k) % NY) for i in range(NY)]) for k in range(1, NY)
    ]
    return [parts[0]] + moved


def local(
    tokens, cotangent, gate_weight, up_weight, down_weight, low_in, low_mid, down_low_in,
    down_low_out, up_order, down_order, up_rows, down_cols, up_count, down_count,
):
    mine = lax.axis_index(MP).astype(I32)
    who = mine.reshape(1)
    low_rows = jnp.concatenate([low_in[:BLK], low_in[BLK:]], axis=1).reshape(32, 4, BLK)
    first = call(
        pack_up_body, shape(PACK_A, 4, BLK), (gate_weight, up_weight, low_mid, low_rows),
        (up_count, who),
    )
    first, down_low_in, down_low_out = together((first, down_low_in, down_low_out))
    dlin_rows = jnp.pad(
        down_low_in.reshape(2, SLOTS, BLK).transpose(1, 0, 2).reshape(2 * SLOTS, BLK), ((0, 4), (0, 0))
    ).reshape(8, 4, BLK)
    dlout_rows = down_low_out.reshape(2, SHARE, BLK).transpose(1, 0, 2).reshape(4, 4, BLK)
    second = call(
        pack_down_body, shape(PACK_B, 4, BLK), (down_weight, dlin_rows, dlout_rows),
        (down_count, who),
    )
    got_up = lax.all_gather(first.reshape(4 * PACK_A, BLK), DP)
    got_down = gather_step(second.reshape(1, 4 * PACK_B, BLK), "zh", 4)
    ids = (mine, up_order, down_order, up_rows, down_cols, up_count, down_count)
    got_down, ids = together((got_down, ids))
    got_down = gather_step(got_down, "x", 4)
    meta = tables(*ids)
    take, take_c, take2_c, give, give2 = permutations()
    got_down, meta = together((got_down, meta))
    got_down = gather_step(got_down, "core", 2)
    tok_t = tokens.reshape(BLK, COLS, BLK).transpose(1, 2, 0)

    slots = shape(SLOTS, BLK, BLK)
    slots_scratch = pltpu.VMEM((SLOTS, BLK, BLK), BF16)
    parcel = shape(NMP, CAP, BLK, BLK)
    got_down, take, give, give2 = together((got_down, take, give, give2))
    back_send, w_d, dlin, dlout = call(
        hidden_grad_body,
        (
            shape(NMP, BACK_ROWS, BLK), shape(LIVE + 1, BLK, BLK), shape(SLOTS, RANK, BLK),
            shape(512, BLK),
        ),
        (got_down, cotangent, take_c, take2_c), (meta,), (slots_scratch,),
    )
    back_send, tok_t = together((back_send, tok_t))
    back_got = lax.all_to_all(back_send, MP, 0, 0, tiled=True)

    hbm = pl.BlockSpec(memory_space=pl.ANY)
    vmem = pl.BlockSpec(memory_space=pltpu.VMEM)
    smem = pl.BlockSpec(memory_space=pltpu.SMEM)
    weights = (LIVE + 1, BLK, 2 * BLK)
    send, act, w_gu, mid, lat, low_share = pl.pallas_call(
        forward_body,
        out_shape=(
            parcel, shape(SLOTS, BLK, 2 * BLK, dtype=F32), shape(*weights), slots,
            shape(BLK, RANK), shape(4, BLK, BLK),
        ),
        in_specs=[smem, hbm, hbm, vmem],
        out_specs=(vmem, vmem, hbm, vmem, vmem, vmem),
        scratch_shapes=[
            slots_scratch, pltpu.VMEM((NDP, 4 * PACK_A, BLK), BF16),
            pltpu.VMEM((BLK, COLS * BLK), BF16), pltpu.VMEM(weights, BF16),
            pltpu.SemaphoreType.DMA((4,)),
        ],
        compiler_params=pltpu.CompilerParams(vmem_limit_bytes=VMEM_LIMIT),
    )(meta, got_up, tokens, take)
    got = lax.all_to_all(send, MP, 0, 0, tiled=True)

    grad_shape = shape(NDP, 4 * GRAD, BLK)
    grad, gu, part_up, back_latent = pl.pallas_call(
        up_grads_body,
        out_shape=(
            grad_shape, shape(SLOTS, BLK, 2 * BLK), shape(BLK, RANK, dtype=F32), shape(BLK, RANK),
        ),
        in_specs=[smem] + [vmem] * 6,
        out_specs=(hbm, vmem, vmem, vmem),
        scratch_shapes=[
            slots_scratch, pltpu.VMEM((NDP, 4 * GRAD_A, BLK), BF16), pltpu.SemaphoreType.DMA,
        ],
        compiler_params=pltpu.CompilerParams(vmem_limit_bytes=VMEM_LIMIT),
    )(meta, back_got, act, mid, lat, tok_t, give)
    grad, hd, part_down = pl.pallas_call(
        down_grads_body,
        out_shape=(grad_shape, slots, shape(BLK, RANK, dtype=F32)),
        in_specs=[smem] + [vmem] * 6 + [hbm],
        out_specs=(hbm, vmem, vmem),
        scratch_shapes=[
            slots_scratch, pltpu.VMEM((SLOTS, RANK, BLK), BF16),
            pltpu.VMEM((NDP, 4 * (GRAD - GRAD_A), BLK), BF16), pltpu.SemaphoreType.DMA,
        ],
        input_output_aliases={7: 0},
        compiler_params=pltpu.CompilerParams(vmem_limit_bytes=VMEM_LIMIT),
    )(meta, got, dlin, back_latent, cotangent, give, give2, grad)
    grad = lax.psum_scatter(
        grad.reshape(NDP * 4 * GRAD, BLK), ("x", "core"), scatter_dimension=0, tiled=True
    )
    part = jnp.concatenate([part_up, part_down], axis=1).astype(BF16)
    parts = spread(part, MP, NMP)
    acc = pltpu.VMEM((COLS, BLK, BLK), F32)
    token_part = call(
        token_part_body, (shape(NY, SHARE, BLK, BLK),) * 2, (gu, w_gu), (meta,), (acc,)
    )
    out_part = call(
        out_part_body, (shape(2, SHARE, BLK, BLK),) * NY, (hd, w_d), (meta,), (acc,)
    )
    parts, token_part, out_part = together((parts, token_part, out_part))
    latents, small = call(
        small_grads_body, (shape(2, BLK, RANK), shape(NDP, 32, BLK)),
        (parts, tok_t, cotangent, give2), (meta,),
    )

    swap = [(0, 1), (1, 0)]
    token_came = lax.ppermute(token_part[1], "zl", swap)
    out_got = rotate(out_part)
    small = lax.all_to_all(small.reshape(8, BLK, BLK), ("x", "core"), 0, 0, tiled=True)
    small = jnp.sum(small.astype(F32), axis=0).astype(BF16).reshape(4, 32, BLK)
    small, grad, token_came, out_got = together((small, grad, token_came, out_got))
    grad = jnp.concatenate([grad.reshape(4, 4 * GRAD, BLK), small], axis=1)
    grad = lax.all_to_all(grad, "zh", 0, 0, tiled=True)
    half = shape(SHARE, BLK, BLK)
    token_got = rotate(call(token_pair_body, (half,) * NY, (token_part[0], token_came), ()))
    out_keep, out_give = call(out_y_body, (half,) * 2, out_got, (meta,))
    out_came = lax.ppermute(out_give, "zl", swap)
    wide = shape(BLK, SHARE * BLK)
    token_grad = call(token_out_body, wide, (*token_got, latents, low_share), ())
    grad, token_grad = together((grad, token_grad))
    small = jnp.sum(grad[:, 4 * GRAD :].astype(F32), axis=0).astype(BF16)
    low_g = spread(small[:16], MP, NMP)
    layer_out = call(layer_out_body, wide, (out_keep, out_came, latents, dlout), ())
    wide = shape(SLOTS, DEPTH, 4, BLK)
    gate_g, up_g, down_g, mid_g, tail = call(
        final_body, (wide, wide, wide, shape(4, SLOTS * BLK), shape(8, 4, BLK)),
        (grad.reshape(4, GRAD + 8, 4, BLK),), (up_count, down_count, who),
        (pltpu.VMEM((GRAD, 4, BLK), BF16),),
    )
    dlin_g = tail.reshape(16, 2, BLK)[:SLOTS].transpose(1, 0, 2).reshape(2, SLOTS * BLK)
    low_g = jnp.concatenate([low_g[:, :, :RANK], low_g[:, :, RANK:]], axis=1)
    low_in_grad = low_g.reshape(2 * BLK, RANK)
    dlout_g = small[16:].reshape(SHARE, 2, BLK).transpose(1, 0, 2).reshape(2, SHARE * BLK)
    return layer_out, token_grad, gate_g, up_g, down_g, low_in_grad, mid_g, dlin_g, dlout_g


def solution(mesh):
    fine = Mesh(mesh.devices.reshape(4, 4, 2, 4, 2), DP + MP)
    rows, both, blocks = P(DP, None), P(DP, MP), P(MP, None, DP, None)
    in_specs = (rows, rows, blocks, blocks, blocks, rows, both, both, both) + (P(),) * 6
    out_specs = (both, both, blocks, blocks, blocks, rows, both, both, both)
    return jax.shard_map(local, mesh=fine, in_specs=in_specs, out_specs=out_specs, check_vma=False)
```
